256 devices in a mesh: dp: 32 (over y, z_hi, core), seq: 8 (over x, z_lo).
Axes of the slice: x: 4, y: 4, z: 8 (z_hi: 4, z_lo: 2; z = z_hi * 2 + z_lo), core: 2. Of those that a mesh axis runs over, the one named last changes fastest.
Arguments:
- qkv_spatial: bfloat16 [32, 16, 64, 3456], P('dp', 'seq'), may hold values from -52 to 52
- tokens: bfloat16 [32, 16, 64, 1152], P('dp', 'seq'), may hold values from -6 to 6
- timesteps: int32 [32], P('dp'), may hold values from 0 to 999
- w_spatial_out: bfloat16 [1152, 1152], P('dp'), may hold values from -0.1875 to 0.1875
- w_temporal_in: bfloat16 [1152, 3456], P('dp'), may hold values from -0.26516504 to 0.26516504
- grad_out: bfloat16 [32, 16, 64, 1152], P('dp', None, 'seq'), may hold values from -2 to 2
Outputs:
- grad_qkv_spatial: bfloat16 [32, 16, 64, 3456], P('dp', 'seq')
- grad_tokens: bfloat16 [32, 16, 64, 1152], P('dp', 'seq')
- grad_w_spatial_out: float32 [1152, 1152], P('dp', 'seq')
- grad_w_temporal_in: float32 [1152, 3456], P('dp', 'seq')
The draws below stay inside these ranges and needn't reach their ends.
All inputs are finite; a program needn't handle non-finite values.
Results may differ from the reference program's by a relative error of at most 0.025.
Values may be sent and summed in bfloat16 or wider, within the bound.
A program may use at most 128 MiB of HBM per device.

```python
import math
import jax
import jax.numpy as jnp
from jax import lax

HEADS = 16
D = 1152
PATCHES = 64
FRAMES = 16
SAMPLES = 32


def draw_qkv_spatial(key, part):
    key = jax.random.fold_in(key, 11)
    first_key = jax.random.fold_in(key, 0)
    full_shape = (SAMPLES, FRAMES, PATCHES, 3, D)
    samples_raw = jnp.clip(jax.random.normal(first_key, full_shape, jnp.float32), -6.0, 6.0)
    return samples_raw.reshape(SAMPLES, FRAMES, PATCHES, 3 * D).astype(jnp.bfloat16)


def draw_w_temporal_in(key, part):
    key = jax.random.fold_in(key, 23)
    spread = D ** (-0.5)
    samples_raw = jnp.clip(jax.random.normal(key, (D, 3 * D), jnp.float32), -6.0, 6.0) * spread
    return samples_raw.astype(jnp.bfloat16)


def place_ends(entries, rng, smallest, largest):
    spot = [jax.random.randint(jax.random.fold_in(rng, axis), (), 0, length) for axis, length in enumerate(entries.shape)]
    widest = entries.shape.index(max(entries.shape))
    next_to = spot[:widest] + [(spot[widest] + 1) % entries.shape[widest]] + spot[widest + 1:]
    return entries.at[tuple(spot)].set(smallest).at[tuple(next_to)].set(largest)


def steps_of(stream_key, dims, cuts, least, top_value):
    def one(axis_at, blocks):
        steps = jax.random.uniform(jax.random.fold_in(jax.random.fold_in(stream_key, 6), axis_at), (blocks,), jnp.float32, least / len(cuts), top_value / len(cuts))
        return jnp.repeat(jnp.exp(steps), dims[axis_at] // blocks).reshape((-1,) + (1,) * (len(dims) - axis_at - 1))

    factor_of = one(*cuts[0])
    for cut in cuts[1:]:
        factor_of = factor_of * one(*cut)
    return factor_of


def noise(stream_key, dims, scale, reach, cuts=(), kind=jnp.bfloat16):
    level = steps_of(stream_key, dims, cuts, -0.22, 0.18) if cuts else 1.0
    result = jax.random.normal(stream_key, dims, jnp.float32) * scale * level
    return jnp.minimum(jnp.maximum(result, -reach), reach).astype(kind)


def setup_inputs(seed: int = 0) -> dict:
    key_of = jax.random.split(jax.random.key(seed), 7)
    return {
        "qkv_spatial": draw_qkv_spatial(jax.random.fold_in(key_of[6], 71), 0),
        "tokens": noise(key_of[1], (SAMPLES, FRAMES, PATCHES, D), 1.0, 6.0, ((0, 32), (1, 8))),
        "timesteps": place_ends(jax.random.randint(key_of[2], (SAMPLES,), 0, 1000), jax.random.fold_in(key_of[2], 1), 0, 999).astype(jnp.int32),
        "w_spatial_out": noise(key_of[3], (D, D), D ** -0.5, 0.1875, ((0, 32),)),
        "w_temporal_in": draw_w_temporal_in(jax.random.fold_in(key_of[6], 71), 0),
        "grad_out": noise(key_of[5], (SAMPLES, FRAMES, PATCHES, D), 0.125, 2.0, ((0, 32), (2, 8))),
    }


def attention_core(packed):
    group_count, positions, packed_width = packed.shape
    head_size = packed_width // (3 * HEADS)
    pieces = packed.astype(jnp.float32).reshape(group_count, positions, 3, HEADS, head_size)
    queries = pieces[:, :, 0]
    key_part = pieces[:, :, 1]
    value_part = pieces[:, :, 2]
    scores = jnp.einsum('gshe,gthe->ghst', queries, key_part, precision=lax.Precision.HIGHEST) * (1.0 / math.sqrt(head_size))
    probs = jax.nn.softmax(scores, axis=-1)
    rounded = lax.optimization_barrier(probs.astype(jnp.bfloat16)).astype(jnp.float32)
    attended = jnp.einsum('ghst,gthe->gshe', rounded, value_part, precision=lax.Precision.HIGHEST)
    return attended.reshape(group_count, positions, HEADS * head_size).astype(jnp.bfloat16)

def time_modulation(timesteps, model_width):
    half_width = model_width // 2
    frequency = jnp.exp(-math.log(10000.0) * jnp.arange(half_width, dtype=jnp.float32) / half_width)
    angles = timesteps.astype(jnp.float32)[:, None] * frequency[None, :]
    cosine = jnp.cos(angles)
    sine = jnp.sin(angles)
    scales = 0.5 * jnp.concatenate([cosine, sine], axis=-1)
    shifts = 0.5 * jnp.concatenate([sine, cosine], axis=-1)
    return (scales, shifts)

def modulate(field_in, scales, shifts):
    values_f = field_in.astype(jnp.float32)
    row_mean = lax.optimization_barrier(jnp.mean(values_f, axis=-1, keepdims=True))
    centred = values_f - row_mean
    row_var = lax.optimization_barrier(jnp.mean(centred * centred, axis=-1, keepdims=True))
    return centred * lax.rsqrt(row_var + 1e-06) * (1.0 + scales) + shifts

def reference(qkv_spatial, tokens, timesteps, w_spatial_out, w_temporal_in, grad_out):
    samples, frame_count, patches, packed_width = qkv_spatial.shape
    model_width = packed_width // 3
    spatial_flat = qkv_spatial.reshape(samples * frame_count, patches, packed_width)
    mixed_out, pull_spatial = jax.vjp(attention_core, spatial_flat)
    mixed_rows = mixed_out.reshape(-1, model_width)
    hidden = (tokens.reshape(-1, model_width).astype(jnp.float32) + jnp.dot(mixed_rows, w_spatial_out, preferred_element_type=jnp.float32)).astype(jnp.bfloat16)
    scales, shifts = time_modulation(timesteps, model_width)

    def norm_field(field_in):
        return modulate(field_in, scales[:, None, :], shifts[:, None, :])
    modulated, pull_norm = jax.vjp(norm_field, hidden.reshape(samples, frame_count * patches, model_width))
    modulated_rows = modulated.astype(jnp.bfloat16).reshape(-1, model_width)
    qkv_temporal = jnp.dot(modulated_rows, w_temporal_in, preferred_element_type=jnp.float32).astype(jnp.bfloat16)
    temporal_flat = qkv_temporal.reshape(samples, frame_count, patches, packed_width).transpose(0, 2, 1, 3).reshape(samples * patches, frame_count, packed_width)
    unused_out, pull_temporal = jax.vjp(attention_core, temporal_flat)
    cotangent = grad_out.transpose(0, 2, 1, 3).reshape(samples * patches, frame_count, model_width)
    grad_flat, = pull_temporal(cotangent)
    grad_temporal = grad_flat.reshape(samples, patches, frame_count, packed_width).transpose(0, 2, 1, 3).reshape(-1, packed_width)
    grad_w_temporal_in = jnp.dot(modulated_rows.T, grad_temporal, preferred_element_type=jnp.float32)
    grad_modulated = jnp.dot(grad_temporal, w_temporal_in.T, preferred_element_type=jnp.float32)
    grad_hidden, = pull_norm(grad_modulated.reshape(samples, frame_count * patches, model_width))
    grad_rows = grad_hidden.reshape(-1, model_width)
    grad_w_spatial_out = jnp.dot(mixed_rows.T, grad_rows, preferred_element_type=jnp.float32)
    grad_mixed = jnp.dot(grad_rows, w_spatial_out.T, preferred_element_type=jnp.float32).astype(jnp.bfloat16)
    grad_spatial, = pull_spatial(grad_mixed.reshape(samples * frame_count, patches, model_width))
    return (grad_spatial.reshape(qkv_spatial.shape), grad_hidden.reshape(tokens.shape), grad_w_spatial_out, grad_w_temporal_in)
```

```python
import functools
import math

import jax
import jax.numpy as jnp
from jax import lax
from jax.experimental import pallas as pl
from jax.experimental.pallas import tpu as pltpu
from jax.sharding import PartitionSpec as P

HEADS = 16
D = 1152
HEAD = D // HEADS
T = 128
NY, NZ, NC, NS = 4, 4, 2, 8
NX = 4
SHARD = 36
MAIN, TAIL = 32, 4
BLOCK = NZ * SHARD
CHUNKS = 4
F32, BF = jnp.float32, jnp.bfloat16
MESH = pl.DeviceIdType.MESH
SCALE = 1.0 / math.sqrt(HEAD)
VMEM = pltpu.VMEM
DMA = pltpu.SemaphoreType.DMA


def contract(a, b, da, db):
    return lax.dot_general(a, b, (((da,), (db,)), ((), ())), preferred_element_type=F32)


def regroup(block):
    return jnp.concatenate(
        [block[64 * f + 8 * p : 64 * f + 8 * p + 8] for p in range(8) for f in range(2)], axis=0
    )


def ungroup(block):
    return jnp.concatenate(
        [block[16 * p + 8 * f : 16 * p + 8 * f + 8] for f in range(2) for p in range(8)], axis=0
    )


def lanes(i, n=128):
    return pl.ds(pl.multiple_of(i * n, 128), n)


def rows8(start, n):
    return pl.ds(pl.multiple_of(start, 8), n)


def loop(n, body, unroll=1):
    lax.fori_loop(0, n, lambda i, c: (body(i), c)[1], 0, unroll=unroll)


def rows_to_t(src, dst, n, group=False):
    def body(j):
        x = src[:, lanes(j)].astype(F32)
        if group:
            x = regroup(x)
        dst[rows8(j * 128, 128), :] = x.T.astype(dst.dtype)

    loop(n // 128, body)


def t_to_rows(src, dst, n):
    def body(j):
        dst[:, lanes(j)] = src[rows8(j * 128, 128), :].T.astype(dst.dtype)

    loop(n // 128, body)


def permute(src, dst):
    def body(y):
        x = src[rows8(y * 288, 288), :]
        parts = []
        for c in range(NC):
            parts += [x[72 * z + 36 * c : 72 * z + 36 * c + 32] for z in range(NZ)]
            parts += [x[72 * z + 36 * c + 32 : 72 * z + 36 * c + 36] for z in range(NZ)]
        dst[rows8(y * 288, 288), :] = jnp.concatenate(parts, axis=0)

    loop(NY, body)


def unpermute(src, dst):
    def body(y):
        x = src[rows8(y * 288, 288), :]
        parts = []
        for z in range(NZ):
            for c in range(NC):
                parts.append(x[144 * c + 32 * z : 144 * c + 32 * z + 32])
                parts.append(x[144 * c + 128 + 4 * z : 144 * c + 128 + 4 * z + 4])
        dst[rows8(y * 288, 288), :] = jnp.concatenate(parts, axis=0)

    loop(NY, body)


def head_slices(ref, h):
    return [ref[rows8(D * i + HEAD * h, HEAD), :].astype(BF) for i in range(3)]


def attend(packed, bias, probs, out):
    def body(h):
        for hh in (2 * h, 2 * h + 1):
            q = packed[rows8(HEAD * hh, HEAD), :].astype(BF)
            k = packed[rows8(D + HEAD * hh, HEAD), :].astype(BF)
            s = contract(k, q, 0, 0) * SCALE + bias[...]
            e = jnp.exp(s - jnp.max(s, axis=0, keepdims=True))
            p = e / jnp.sum(e, axis=0, keepdims=True)
            probs[hh] = p
            if out is not None:
                v = packed[rows8(2 * D + HEAD * hh, HEAD), :].astype(BF)
                o = contract(v, p.astype(BF), 1, 0)
                out[rows8(HEAD * hh, HEAD), :] = o.astype(BF).astype(F32)

    loop(HEADS // 2, body)


def attend_back(packed, probs, cot, grad):
    def body(h):
        for hh in (2 * h, 2 * h + 1):
            q, k, v = head_slices(packed, hh)
            do = cot[rows8(HEAD * hh, HEAD), :].astype(BF)
            p = probs[hh]
            dp = contract(v, do, 0, 0).astype(BF).astype(F32)
            dv = contract(do, p.astype(BF), 1, 1)
            ds = p * (dp - jnp.sum(dp * p, axis=0, keepdims=True)) * SCALE
            ds = ds.astype(BF)
            dq = contract(k, ds, 1, 0)
            dk = contract(q, ds, 1, 1)
            grad[rows8(HEAD * hh, HEAD), :] = dq
            grad[rows8(D + HEAD * hh, HEAD), :] = dk
            grad[rows8(2 * D + HEAD * hh, HEAD), :] = dv

    loop(HEADS // 2, body)


def kernel(
    qkv, tokens, gout, wo, wi, tail, sc, sh,
    out_qkv, out_tok, out_gwo, out_gwi,
    w, tails, packed, spat, probs, probs_t, bias, grad, grad_b, ft, fp, rows_b, rows_t, hid, hid_in, g_out,
    xhat, rstd, mixed_all, mod_all, gt_all, g_all, cot, g_in, gt_b,
    gwi_y, gwo_y, gwi_yin, gwo_yin, gwi_z, gwo_z, gwi_zin, gwo_zin,
    z_s, z_r, t_s, t_r, y_s, y_r, c_s, c_r, mx_s, mx_r, md_s, md_r,
    h_s, h_r, g_s, g_r, gt_s, gt_r, gc_s, gc_r, ri_s, ri_r, ro_s, ro_r, si_s, si_r, so_s, so_r,
):
    d = lax.axis_index("dp")
    s = lax.axis_index("seq")
    y, u = d // 8, d % 8
    z, c = u // 2, u % 2
    x, zl = s // 2, s % 2
    mine = y * 2 + c

    def z_peer(k):
        return (y * 8 + lax.rem(z + k, NZ) * 2 + c, s)

    def y_peer(k):
        return (lax.rem(y + k, NY) * 8 + u, s)

    core_peer = (d + 1 - 2 * c, s)

    def u_peer(k):
        return (y * 8 + lax.rem(u + k, 8), s)

    def x_peer(k):
        return (d, lax.rem(x + k, NX) * 2 + zl)

    pair = (d, s + 1 - 2 * zl)

    def s_peer(k):
        return (d, lax.rem(s + k, NS))

    peers = (
        [z_peer(k) for k in range(1, NZ)]
        + [y_peer(k) for k in range(1, NY)]
        + [u_peer(k) for k in range(1, 8)]
        + [s_peer(k) for k in range(1, NS)]
    )
    peers = peers[3:]
    barrier = pltpu.get_barrier_semaphore()
    for p in peers:
        pl.semaphore_signal(barrier, inc=1, device_id=p, device_id_type=MESH)

    started = []

    def copy(src, dst, ss, rs, to):
        return pltpu.make_async_remote_copy(
            src_ref=src, dst_ref=dst, send_sem=ss, recv_sem=rs, device_id=to, device_id_type=MESH
        )

    def go(cp):
        cp.start()
        started.append(cp)

    def w_main(q):
        if q == 0:
            return wo.at[pl.ds(0, MAIN), :]
        return wi.at[pl.ds(0, MAIN), pl.ds((q - 1) * D, D)]

    def z_copy(q, k):
        return copy(
            w_main(q), w.at[q, mine, pl.ds(pl.multiple_of(z * MAIN, 16), MAIN), :],
            z_s.at[q, k - 1], z_r.at[q, k - 1], z_peer(k),
        )

    def t_copy(k):
        return copy(tail, tails.at[z], t_s.at[k - 1], t_r.at[k - 1], z_peer(k))

    def y_copy(q, k):
        return copy(w.at[q, mine], w.at[q, mine], y_s.at[q, k - 1], y_r.at[q, k - 1], y_peer(k))

    def c_copy(q, k):
        blk = lax.rem(y + NY - k, NY) * 2 + c
        return copy(w.at[q, blk], w.at[q, blk], c_s.at[q, k], c_r.at[q, k], core_peer)

    def gather_pair(buf, ss, rs):
        return copy(buf.at[:, lanes(s)], buf.at[:, lanes(s)], ss.at[0], rs.at[0], pair)

    def gather_x(buf, ss, rs, k, other):
        slot = s + (1 - 2 * zl) * other
        i = k + 3 * other
        return copy(buf.at[:, lanes(slot)], buf.at[:, lanes(slot)], ss.at[i], rs.at[i], x_peer(k))

    def rows_copy(src, dst, ss, rs, k):
        to = lax.rem(s + k, NS)
        return copy(
            src.at[pl.ds(pl.multiple_of(to * 16, 16), 16), :],
            dst.at[pl.ds(pl.multiple_of(s * 16, 16), 16), :],
            ss.at[k - 1], rs.at[k - 1], s_peer(k),
        )

    def cols_copy(src, dst, n, ss, rs, k):
        to = lax.rem(s + k, NS)
        return copy(
            src.at[pl.ds(pl.multiple_of(to * n, 16), n), :], dst.at[:, lanes(s)],
            ss.at[k - 1], rs.at[k - 1], s_peer(k),
        )

    def sum_y(src, dst, ss, rs, k):
        return copy(src.at[lax.rem(y + k, NY)], dst.at[k - 1], ss.at[k - 1], rs.at[k - 1], y_peer(k))

    def sum_z(src, dst, ss, rs, k):
        return copy(src.at[lax.rem(u + k, 8)], dst.at[k - 1], ss.at[k - 1], rs.at[k - 1], u_peer(k))

    for q in range(CHUNKS):
        w[q, mine, pl.ds(pl.multiple_of(z * MAIN, 16), MAIN), :] = w_main(q)[...]
    tails[z] = tail[...]
    pl.semaphore_wait(barrier, len(peers))

    for k in range(1, NZ):
        go(t_copy(k))
    for q in range(CHUNKS):
        for k in range(1, NZ):
            go(z_copy(q, k))

    rows_to_t(qkv, spat, 3 * D, group=True)
    ki = lax.broadcasted_iota(jnp.int32, (T, T), 0)
    qi = lax.broadcasted_iota(jnp.int32, (T, T), 1)
    bias[...] = jnp.where((ki // 8) % 2 == (qi // 8) % 2, 0.0, -1e30).astype(F32)
    attend(spat, bias, probs, ft)
    mixed_all[:, lanes(s)] = ft[...].astype(BF)
    go(gather_pair(mixed_all, mx_s, mx_r))
    permute(ft, fp)
    t_to_rows(fp, rows_b, D)
    bias[...] = jnp.where(ki % 8 == qi % 8, 0.0, -1e30).astype(F32)
    rows_to_t(gout, cot, D)

    for k in range(1, NZ):
        t_copy(k).wait_recv()

    low = lax.broadcasted_iota(jnp.int32, (8, 128), 0) < 4

    def tail_body(m):
        full = [tails[zz, pl.ds(pl.multiple_of(m * 16, 16), 16), :].astype(F32) for zz in range(NZ)]
        for half in range(2):
            a = [v[8 * half : 8 * half + 8] for v in full]
            r = [pltpu.roll(v, 4, 0) for v in a]
            even = [jnp.where(low, a[0], r[1]), jnp.where(low, a[2], r[3])]
            odd = [jnp.where(low, r[0], a[1]), jnp.where(low, r[2], a[3])]
            for i, pieces in enumerate((even, odd)):
                j = 4 * m + 2 * half + i
                w[j // 9, mine, pl.ds(NZ * MAIN, 16), lanes(j % 9)] = jnp.concatenate(pieces, axis=0).astype(BF)

    loop(9, tail_body)

    def spread(q):
        for k in range(1, NZ):
            z_copy(q, k).wait_recv()
        for k in range(1, NY):
            go(y_copy(q, k))
        go(c_copy(q, 0))

    def relay(q):
        for k in range(1, NY):
            y_copy(q, k).wait_recv()
            go(c_copy(q, k))

    def arrived(q):
        for k in range(NY):
            c_copy(q, k).wait_recv()

    def fan_out(buf, ss, rs):
        gather_pair(buf, ss, rs).wait_recv()
        for k in range(1, NX):
            go(gather_x(buf, ss, rs, k, 0))
            go(gather_x(buf, ss, rs, k, 1))

    def fanned(buf, ss, rs):
        for k in range(1, NX):
            gather_x(buf, ss, rs, k, 0).wait_recv()
            gather_x(buf, ss, rs, k, 1).wait_recv()

    spread(0)
    fan_out(mixed_all, mx_s, mx_r)
    spread(1)
    relay(0)
    arrived(0)

    def hidden_body(n):
        tok = regroup(tokens[:, lanes(n, 384)].astype(F32))
        acc = contract(rows_b[...], w[0, :, :, lanes(n, 384)].reshape(D, 384), 1, 0)
        hid[:, lanes(n, 384)] = (tok + acc).astype(BF)

    loop(3, hidden_body)
    own = pl.ds(pl.multiple_of(s * 16, 16), 16)
    hid_in[own, :] = hid[own, :]
    for k in range(1, NS):
        go(rows_copy(hid, hid_in, h_s, h_r, k))
    spread(2)
    for k in range(1, NS):
        rows_copy(hid, hid_in, h_s, h_r, k).wait_recv()

    hf = hid_in[...].astype(F32)
    centred = hf - jnp.mean(hf, axis=-1, keepdims=True)
    inv = lax.rsqrt(jnp.mean(centred * centred, axis=-1, keepdims=True) + 1e-06)
    xh = centred * inv
    xhat[...] = xh
    rstd[...] = jnp.broadcast_to(inv, (T, 128))
    rows_t[...] = (xh * sc[...] + sh[...]).astype(BF).astype(F32)
    rows_to_t(rows_t, ft, D)
    mod_all[:, lanes(s)] = ft[...].astype(BF)
    go(gather_pair(mod_all, md_s, md_r))
    permute(ft, fp)
    t_to_rows(fp, rows_b, D)
    spread(3)
    fan_out(mod_all, md_s, md_r)

    def project(q):
        relay(q)
        arrived(q)

        def body(n):
            acc = contract(rows_b[...], w[q, :, :, lanes(n, 384)].reshape(D, 384), 1, 0)
            acc = acc.astype(BF).astype(F32)
            packed[rows8((q - 1) * D + n * 384, 384), :] = acc.T

        loop(3, body)

    project(1)
    project(2)
    attend(packed, bias, probs_t, None)
    project(3)
    attend_back(packed, probs_t, cot, grad)
    grad_b[...] = grad[...].astype(BF)
    gt_all[:, lanes(s)] = grad_b[pl.ds(pl.multiple_of(s * 432, 16), 432), :]
    for k in range(1, NS):
        go(cols_copy(grad_b, gt_all, 432, gt_s, gt_r, k))

    def back_body(b):
        acc = jnp.zeros((2 * BLOCK, T), F32)
        for q in range(1, CHUNKS):
            acc += contract(w[q, pl.ds(2 * b, 2)].reshape(2 * BLOCK, D), grad_b[pl.ds((q - 1) * D, D), :], 1, 0)
        fp[rows8(b * 2 * BLOCK, 2 * BLOCK), :] = acc

    loop(NY, back_body)
    unpermute(fp, ft)
    t_to_rows(ft, rows_t, D)
    dx = rows_t[...] * sc[...]
    xh = xhat[...]
    m1 = jnp.mean(dx, axis=-1, keepdims=True)
    m2 = jnp.mean(dx * xh, axis=-1, keepdims=True)
    g_out[...] = (rstd[:, 0:1] * (dx - m1 - xh * m2)).astype(BF)
    g_in[own, :] = g_out[own, :]
    for k in range(1, NS):
        go(rows_copy(g_out, g_in, g_s, g_r, k))
    for k in range(1, NS):
        rows_copy(g_out, g_in, g_s, g_r, k).wait_recv()

    def tok_body(j):
        v = g_in[:, lanes(j)].astype(F32)
        out_tok[:, lanes(j)] = ungroup(v).astype(BF)
        gt_b[rows8(j * 128, 128), :] = v.T.astype(BF)

    loop(9, tok_body)
    g_all[:, lanes(s)] = gt_b[pl.ds(pl.multiple_of(s * 144, 16), 144), :]
    for k in range(1, NS):
        go(cols_copy(gt_b, g_all, 144, gc_s, gc_r, k))

    def mixed_body(b):
        fp[rows8(b * 2 * BLOCK, 2 * BLOCK), :] = contract(
            w[0, pl.ds(2 * b, 2)].reshape(2 * BLOCK, D), gt_b[...], 1, 0
        )

    loop(NY, mixed_body)
    unpermute(fp, ft)

    fanned(mod_all, md_s, md_r)
    for k in range(1, NS):
        cols_copy(grad_b, gt_all, 432, gt_s, gt_r, k).wait_recv()

    def gwi_body(b):
        gwi_y[b] = contract(mod_all[rows8(b * 288, 288), :], gt_all[...], 1, 1).astype(BF)

    loop(NY, gwi_body)
    for k in range(1, NY):
        go(sum_y(gwi_y, gwi_yin, ri_s, ri_r, k))

    fanned(mixed_all, mx_s, mx_r)
    for k in range(1, NS):
        cols_copy(gt_b, g_all, 144, gc_s, gc_r, k).wait_recv()

    def gwo_body(b):
        gwo_y[b] = contract(mixed_all[rows8(b * 288, 288), :], g_all[...], 1, 1).astype(BF)

    loop(NY, gwo_body)
    for k in range(1, NY):
        go(sum_y(gwo_y, gwo_yin, ro_s, ro_r, k))

    def add_y(src, dst, ss, rs, out):
        for k in range(1, NY):
            sum_y(src, dst, ss, rs, k).wait_recv()
        acc = src[y].astype(F32)
        for k in range(1, NY):
            acc += dst[k - 1].astype(F32)
        for i in range(8):
            out[i, 0:SHARD, :] = acc[SHARD * i : SHARD * i + SHARD].astype(BF)
            out[i, SHARD:48, :] = jnp.zeros((48 - SHARD, acc.shape[1]), BF)

    def add_z(src, dst, ss, rs, out):
        for k in range(1, 8):
            sum_z(src, dst, ss, rs, k).wait_recv()
        acc = src[u].astype(F32)
        for k in range(1, 8):
            acc += dst[k - 1].astype(F32)
        out[...] = acc[0:SHARD]

    attend_back(spat, probs, ft, grad)
    add_y(gwi_y, gwi_yin, ri_s, ri_r, gwi_z)
    for k in range(1, 8):
        go(sum_z(gwi_z, gwi_zin, si_s, si_r, k))
    add_y(gwo_y, gwo_yin, ro_s, ro_r, gwo_z)
    for k in range(1, 8):
        go(sum_z(gwo_z, gwo_zin, so_s, so_r, k))

    def out_body(j):
        out_qkv[:, lanes(j)] = ungroup(grad[rows8(j * 128, 128), :].T).astype(BF)

    loop(27, out_body)
    add_z(gwi_z, gwi_zin, si_s, si_r, out_gwi)
    add_z(gwo_z, gwo_zin, so_s, so_r, out_gwo)
    for cp in started:
        cp.wait_send()


def time_modulation(timesteps):
    half = D // 2
    frequency = jnp.exp(-math.log(10000.0) * jnp.arange(half, dtype=F32) / half)
    angles = timesteps.astype(F32)[:, None] * frequency[None, :]
    cosine, sine = jnp.cos(angles), jnp.sin(angles)
    return (
        1.0 + 0.5 * jnp.concatenate([cosine, sine], axis=-1),
        0.5 * jnp.concatenate([sine, cosine], axis=-1),
    )


def shards(qkv_spatial, tokens, timesteps, w_out, w_in, grad_out):
    sc, sh = time_modulation(timesteps)
    tail = jnp.concatenate([w_out[MAIN:], w_in[MAIN:]], axis=1)
    tail = tail.reshape(TAIL, 36, 128).transpose(1, 0, 2).reshape(144, 128)
    dma = lambda *n: DMA(n)
    scratch = [
        VMEM((CHUNKS, NY * NC, BLOCK, D), BF),
        VMEM((NZ, 144, 128), BF),
        VMEM((3 * D, T), F32),
        VMEM((3 * D, T), F32),
        VMEM((HEADS, T, T), F32),
        VMEM((HEADS, T, T), F32),
        VMEM((T, T), F32),
        VMEM((3 * D, T), F32),
        VMEM((3 * D, T), BF),
        VMEM((D, T), F32),
        VMEM((D, T), F32),
        VMEM((T, D), BF),
        VMEM((T, D), F32),
        VMEM((T, D), BF),
        VMEM((T, D), BF),
        VMEM((T, D), BF),
        VMEM((T, D), F32),
        VMEM((T, 128), F32),
        VMEM((D, NS * T), BF),
        VMEM((D, NS * T), BF),
        VMEM((432, NS * T), BF),
        VMEM((144, NS * T), BF),
        VMEM((D, T), F32),
        VMEM((T, D), BF),
        VMEM((D, T), BF),
        VMEM((NY, 288, 432), BF),
        VMEM((NY, 288, 144), BF),
        VMEM((3, 288, 432), BF),
        VMEM((3, 288, 144), BF),
        VMEM((8, 48, 432), BF),
        VMEM((8, 48, 144), BF),
        VMEM((7, 48, 432), BF),
        VMEM((7, 48, 144), BF),
        dma(4, 3), dma(4, 3), dma(3), dma(3), dma(4, 3), dma(4, 3), dma(4, 4), dma(4, 4),
        dma(7), dma(7), dma(7), dma(7),
        dma(7), dma(7), dma(7), dma(7), dma(7), dma(7), dma(7), dma(7),
        dma(3), dma(3), dma(3), dma(3), dma(7), dma(7), dma(7), dma(7),
    ]
    spec = pl.BlockSpec(memory_space=VMEM)
    gq, gt, gwo, gwi = pl.pallas_call(
        kernel,
        out_shape=(
            jax.ShapeDtypeStruct((T, 3 * D), BF),
            jax.ShapeDtypeStruct((T, D), BF),
            jax.ShapeDtypeStruct((SHARD, 144), F32),
            jax.ShapeDtypeStruct((SHARD, 432), F32),
        ),
        in_specs=[spec] * 8,
        out_specs=(spec,) * 4,
        scratch_shapes=scratch,
        compiler_params=pltpu.CompilerParams(
            collective_id=0, has_side_effects=True, vmem_limit_bytes=60 * 1024 * 1024
        ),
    )(
        qkv_spatial.reshape(T, 3 * D), tokens.reshape(T, D), grad_out.reshape(T, D),
        w_out, w_in, tail, sc, sh,
    )
    return gq.reshape(qkv_spatial.shape), gt.reshape(tokens.shape), gwo, gwi


def solution(mesh):
    placed = (
        P("dp", "seq", None, None),
        P("dp", "seq", None, None),
        P("dp"),
        P("dp", None),
        P("dp", None),
        P("dp", None, "seq", None),
    )
    return jax.shard_map(
        shards,
        mesh=mesh,
        in_specs=placed,
        out_specs=(
            P("dp", "seq", None, None),
            P("dp", "seq", None, None),
            P("dp", "seq"),
            P("dp", "seq"),
        ),
        check_vma=False,
    )
```

```python
import functools
import math

import jax
import jax.numpy as jnp
from jax import lax
from jax.experimental import pallas as pl
from jax.experimental.pallas import tpu as pltpu
from jax.sharding import PartitionSpec as P

HEADS = 16
D = 1152
HEAD = D // HEADS
T = 128
NY, NZ, NC, NS = 4, 4, 2, 8
NX = 4
SHARD = 36
MAIN, TAIL = 32, 4
BLOCK = NZ * SHARD
CHUNKS = 4
F32, BF = jnp.float32, jnp.bfloat16
MESH = pl.DeviceIdType.MESH
SCALE = 1.0 / math.sqrt(HEAD)
VMEM = pltpu.VMEM
DMA = pltpu.SemaphoreType.DMA


def contract(a, b, da, db):
    return lax.dot_general(a, b, (((da,), (db,)), ((), ())), preferred_element_type=F32)


def regroup(block):
    return jnp.concatenate(
        [block[64 * f + 8 * p : 64 * f + 8 * p + 8] for p in range(8) for f in range(2)], axis=0
    )


def ungroup(block):
    return jnp.concatenate(
        [block[16 * p + 8 * f : 16 * p + 8 * f + 8] for f in range(2) for p in range(8)], axis=0
    )


def lanes(i, n=128):
    return pl.ds(pl.multiple_of(i * n, 128), n)


def rows8(start, n):
    return pl.ds(pl.multiple_of(start, 8), n)


def loop(n, body, unroll=1):
    lax.fori_loop(0, n, lambda i, c: (body(i), c)[1], 0, unroll=unroll)


def rows_to_t(src, dst, n, group=False):
    def body(j):
        x = src[:, lanes(j)].astype(F32)
        if group:
            x = regroup(x)
        dst[rows8(j * 128, 128), :] = x.T.astype(dst.dtype)

    loop(n // 128, body)


def t_to_rows(src, dst, n):
    def body(j):
        dst[:, lanes(j)] = src[rows8(j * 128, 128), :].T.astype(dst.dtype)

    loop(n // 128, body)


def permute(src, dst):
    def body(y):
        x = src[rows8(y * 288, 288), :]
        for c in range(NC):
            parts = [x[72 * z + 36 * c : 72 * z + 36 * c + 32] for z in range(NZ)]
            parts += [x[72 * z + 36 * c + 32 : 72 * z + 36 * c + 36] for z in range(NZ)]
            dst[rows8(576 * c + y * 144, 144), :] = jnp.concatenate(parts, axis=0)

    loop(NY, body)


def unpermute(src, dst):
    def body(y):
        x = [src[rows8(576 * c + y * 144, 144), :] for c in range(NC)]
        parts = []
        for z in range(NZ):
            for c in range(NC):
                parts.append(x[c][32 * z : 32 * z + 32])
                parts.append(x[c][128 + 4 * z : 128 + 4 * z + 4])
        dst[rows8(y * 288, 288), :] = jnp.concatenate(parts, axis=0)

    loop(NY, body)


def head_slices(ref, h):
    return [ref[rows8(D * i + HEAD * h, HEAD), :].astype(BF) for i in range(3)]


def attend(packed, bias, probs, out):
    def body(h):
        for hh in (2 * h, 2 * h + 1):
            q = packed[rows8(HEAD * hh, HEAD), :].astype(BF)
            k = packed[rows8(D + HEAD * hh, HEAD), :].astype(BF)
            s = contract(k, q, 0, 0) * SCALE + bias[...]
            e = jnp.exp(s - jnp.max(s, axis=0, keepdims=True))
            p = e / jnp.sum(e, axis=0, keepdims=True)
            probs[hh] = p
            if out is not None:
                v = packed[rows8(2 * D + HEAD * hh, HEAD), :].astype(BF)
                o = contract(v, p.astype(BF), 1, 0)
                out[rows8(HEAD * hh, HEAD), :] = o.astype(BF).astype(F32)

    loop(HEADS // 2, body)


def attend_back(packed, probs, cot, grad, first=0, count=HEADS):
    def body(h):
        h = h + first // 2
        for hh in (2 * h, 2 * h + 1):
            q, k, v = head_slices(packed, hh)
            do = cot[rows8(HEAD * hh, HEAD), :].astype(BF)
            p = probs[hh]
            dp = contract(v, do, 0, 0).astype(BF).astype(F32)
            dv = contract(do, p.astype(BF), 1, 1)
            ds = p * (dp - jnp.sum(dp * p, axis=0, keepdims=True)) * SCALE
            ds = ds.astype(BF)
            dq = contract(k, ds, 1, 0)
            dk = contract(q, ds, 1, 1)
            grad[rows8(HEAD * hh, HEAD), :] = dq
            grad[rows8(D + HEAD * hh, HEAD), :] = dk
            grad[rows8(2 * D + HEAD * hh, HEAD), :] = dv

    loop(count // 2, body)


def kernel(
    qkv, tokens, gout, wo, wi, tail, sc, sh,
    out_qkv, out_tok, out_gwo, out_gwi,
    w, tails, packed, spat, probs, probs_t, bias, grad, grad_b, ft, fp, rows_b, rows_t, hid, hid_in, g_out,
    xhat, rstd, mixed_all, mod_all, gt_all, g_all, cot, g_in, gt_b,
    gwi_p, gwi_c, gwi_h, gwi_y, gwi_t, gwi_z, gwo_p, gwo_c, gwo_h, gwo_y, gwo_t, gwo_z,
    z_s, z_r, t_s, t_r, y_s, y_r, c_s, c_r, mx_s, mx_r, md_s, md_r,
    h_s, h_r, g_s, g_r, gt_s, gt_r, gc_s, gc_r, ri_s, ri_r, ro_s, ro_r,
):
    d = lax.axis_index("dp")
    s = lax.axis_index("seq")
    y, u = d // 8, d % 8
    z, c = u // 2, u % 2
    x, zl = s // 2, s % 2
    mine = c * NY + y

    def z_peer(k):
        return (y * 8 + lax.rem(z + k, NZ) * 2 + c, s)

    def y_peer(k):
        return (lax.rem(y + k, NY) * 8 + u, s)

    core_peer = (d + 1 - 2 * c, s)

    def u_peer(k):
        return (y * 8 + lax.rem(u + k, 8), s)

    def x_peer(k):
        return (d, lax.rem(x + k, NX) * 2 + zl)

    pair = (d, s + 1 - 2 * zl)

    def s_peer(k):
        return (d, lax.rem(s + k, NS))

    peers = (
        [z_peer(k) for k in range(1, NZ)]
        + [y_peer(k) for k in range(1, NY)]
        + [u_peer(k) for k in range(1, 8)]
        + [s_peer(k) for k in range(1, NS)]
    )
    peers = peers[3:]
    barrier = pltpu.get_barrier_semaphore()
    for p in peers:
        pl.semaphore_signal(barrier, inc=1, device_id=p, device_id_type=MESH)

    started = []

    def copy(src, dst, ss, rs, to):
        return pltpu.make_async_remote_copy(
            src_ref=src, dst_ref=dst, send_sem=ss, recv_sem=rs, device_id=to, device_id_type=MESH
        )

    def go(cp):
        cp.start()
        started.append(cp)

    def w_main(q):
        if q == 0:
            return wo.at[pl.ds(0, MAIN), :]
        return wi.at[pl.ds(0, MAIN), pl.ds((q - 1) * D, D)]

    def z_copy(q, k):
        return copy(
            w_main(q), w.at[q, mine, pl.ds(pl.multiple_of(z * MAIN, 16), MAIN), :],
            z_s.at[q, k - 1], z_r.at[q, k - 1], z_peer(k),
        )

    def t_copy(k):
        return copy(tail, tails.at[z], t_s.at[k - 1], t_r.at[k - 1], z_peer(k))

    def block(k):
        return c * NY + lax.rem(y + NY + k, NY)

    def y_copy(q, i):
        part = w.at[q, mine]
        if i == 2:
            part = w.at[q, block(-1), pl.ds(0, 80), :]
        if i == 3:
            part = w.at[q, block(1), pl.ds(80, 64), :]
        return copy(part, part, y_s.at[q, i], y_r.at[q, i], y_peer(1 if i % 2 == 0 else 3))

    def c_copy(q, i):
        part = w.at[q, block((0, -1, 1, 2)[i])]
        return copy(part, part, c_s.at[q, i], c_r.at[q, i], core_peer)

    def gather_copy(buf, ss, rs, i):
        if i == 0:
            part, to = buf.at[:, lanes(s)], pair
        elif i < 3:
            part, to = buf.at[:, lanes(x, 256)], x_peer(1 if i == 1 else 3)
        elif i == 3:
            part, to = buf.at[:, lanes(2 * lax.rem(x + 3, NX))], x_peer(1)
        else:
            part, to = buf.at[:, lanes(2 * lax.rem(x + 1, NX) + 1)], x_peer(3)
        return copy(part, part, ss.at[i], rs.at[i], to)

    def rows_copy(src, dst, ss, rs, k):
        to = lax.rem(s + k, NS)
        return copy(
            src.at[pl.ds(pl.multiple_of(to * 16, 16), 16), :],
            dst.at[pl.ds(pl.multiple_of(s * 16, 16), 16), :],
            ss.at[k - 1], rs.at[k - 1], s_peer(k),
        )

    def cols_copy(src, dst, n, ss, rs, k):
        to = lax.rem(s + k, NS)
        return copy(
            src.at[pl.ds(pl.multiple_of(to * n, 16), n), :], dst.at[:, lanes(s)],
            ss.at[k - 1], rs.at[k - 1], s_peer(k),
        )

    def sum_c(part, got, ss, rs):
        return copy(
            part.at[:, pl.ds(pl.multiple_of((1 - c) * 144, 16), 144), :], got, ss.at[0], rs.at[0], core_peer
        )

    def sum_y(half, got, ss, rs, k):
        return copy(half.at[lax.rem(y + k, NY)], got.at[k - 1], ss.at[k], rs.at[k], y_peer(k))

    def sum_z(slab, got, ss, rs, j):
        return copy(slab.at[j], got.at[z], ss.at[4 + j], rs.at[4 + z], (y * 8 + 4 * c + j, s))

    def add_c(part, got, half, ygot, ss, rs):
        sum_c(part, got, ss, rs).wait_recv()

        def body(b):
            own_half = part[b, pl.ds(pl.multiple_of(c * 144, 16), 144), :].astype(F32)
            half[b] = (own_half + got[b].astype(F32)).astype(BF)

        loop(NY, body)
        for k in range(1, NY):
            go(sum_y(half, ygot, ss, rs, k))

    def add_y(half, got, slab, zgot, ss, rs):
        for k in range(1, NY):
            sum_y(half, got, ss, rs, k).wait_recv()
        acc = half[y].astype(F32)
        for k in range(1, NY):
            acc += got[k - 1].astype(F32)
        for j in range(4):
            slab[j, 0:SHARD, :] = acc[SHARD * j : SHARD * j + SHARD].astype(BF)
            slab[j, SHARD:48, :] = jnp.zeros((48 - SHARD, acc.shape[1]), BF)
        for j in range(4):
            @pl.when(4 * c + j != u)
            def _():
                sum_z(slab, zgot, ss, rs, j).start()

            @pl.when(4 * c + j == u)
            def _():
                zgot[z] = slab[j]

    def add_z(slab, zgot, ss, rs, out):
        for zz in range(NZ):
            @pl.when((zz != z) | (u // 4 != c))
            def _():
                copy(slab.at[0], zgot.at[zz], ss.at[4], rs.at[4 + zz], core_peer).wait_recv()
        acc = zgot[0].astype(F32)
        for zz in range(1, NZ):
            acc += zgot[zz].astype(F32)
        out[...] = acc[0:SHARD]
        for j in range(4):
            @pl.when(4 * c + j != u)
            def _():
                sum_z(slab, zgot, ss, rs, j).wait_send()

    for q in range(CHUNKS):
        w[q, mine, pl.ds(pl.multiple_of(z * MAIN, 16), MAIN), :] = w_main(q)[...]
    tails[z] = tail[...]
    pl.semaphore_wait(barrier, len(peers))

    for k in range(1, NZ):
        go(t_copy(k))
    for q in range(CHUNKS):
        for k in range(1, NZ):
            go(z_copy(q, k))

    rows_to_t(qkv, spat, 3 * D, group=True)
    ki = lax.broadcasted_iota(jnp.int32, (T, T), 0)
    qi = lax.broadcasted_iota(jnp.int32, (T, T), 1)
    bias[...] = jnp.where((ki // 8) % 2 == (qi // 8) % 2, 0.0, -1e30).astype(F32)
    attend(spat, bias, probs, ft)
    mixed_all[:, lanes(s)] = ft[...].astype(BF)
    go(gather_copy(mixed_all, mx_s, mx_r, 0))
    permute(ft, fp)
    t_to_rows(fp, rows_b, D)
    bias[...] = jnp.where(ki % 8 == qi % 8, 0.0, -1e30).astype(F32)
    rows_to_t(gout, cot, D)

    for k in range(1, NZ):
        t_copy(k).wait_recv()

    low = lax.broadcasted_iota(jnp.int32, (8, 128), 0) < 4

    def tail_body(m):
        full = [tails[zz, pl.ds(pl.multiple_of(m * 16, 16), 16), :].astype(F32) for zz in range(NZ)]
        for half in range(2):
            a = [v[8 * half : 8 * half + 8] for v in full]
            r = [pltpu.roll(v, 4, 0) for v in a]
            even = [jnp.where(low, a[0], r[1]), jnp.where(low, a[2], r[3])]
            odd = [jnp.where(low, r[0], a[1]), jnp.where(low, r[2], a[3])]
            for i, pieces in enumerate((even, odd)):
                j = 4 * m + 2 * half + i
                w[j // 9, mine, pl.ds(NZ * MAIN, 16), lanes(j % 9)] = jnp.concatenate(pieces, axis=0).astype(BF)

    loop(9, tail_body)

    def spread(q):
        for k in range(1, NZ):
            z_copy(q, k).wait_recv()
        go(y_copy(q, 0))
        go(y_copy(q, 1))
        go(c_copy(q, 0))

    def relay(q):
        for i in range(2):
            y_copy(q, i).wait_recv()
            go(y_copy(q, 2 + i))
            go(c_copy(q, 1 + i))

    def complete(q):
        for i in range(2):
            y_copy(q, 2 + i).wait_recv()
        go(c_copy(q, 3))
        for i in range(4):
            c_copy(q, i).wait_recv()

    def fan_out(buf, ss, rs):
        gather_copy(buf, ss, rs, 0).wait_recv()
        for i in (1, 2):
            go(gather_copy(buf, ss, rs, i))

    def pass_on(buf, ss, rs):
        for i in (1, 2):
            gather_copy(buf, ss, rs, i).wait_recv()
            go(gather_copy(buf, ss, rs, 2 + i))

    def fanned(buf, ss, rs):
        for i in (3, 4):
            gather_copy(buf, ss, rs, i).wait_recv()

    spread(0)
    fan_out(mixed_all, mx_s, mx_r)
    relay(0)
    spread(1)
    complete(0)

    def hidden_body(n):
        tok = regroup(tokens[:, lanes(n, 384)].astype(F32))
        acc = contract(rows_b[...], w[0, :, :, lanes(n, 384)].reshape(D, 384), 1, 0)
        hid[:, lanes(n, 384)] = (tok + acc).astype(BF)

    loop(3, hidden_body)
    own = pl.ds(pl.multiple_of(s * 16, 16), 16)
    hid_in[own, :] = hid[own, :]
    for k in range(1, NS):
        go(rows_copy(hid, hid_in, h_s, h_r, k))
    pass_on(mixed_all, mx_s, mx_r)
    relay(1)
    spread(2)
    for k in range(1, NS):
        rows_copy(hid, hid_in, h_s, h_r, k).wait_recv()

    hf = hid_in[...].astype(F32)
    centred = hf - jnp.mean(hf, axis=-1, keepdims=True)
    inv = lax.rsqrt(jnp.mean(centred * centred, axis=-1, keepdims=True) + 1e-06)
    xh = centred * inv
    xhat[...] = xh
    rstd[...] = jnp.broadcast_to(inv, (T, 128))
    rows_t[...] = (xh * sc[...] + sh[...]).astype(BF).astype(F32)
    rows_to_t(rows_t, ft, D)
    mod_all[:, lanes(s)] = ft[...].astype(BF)
    go(gather_copy(mod_all, md_s, md_r, 0))
    permute(ft, fp)
    t_to_rows(fp, rows_b, D)
    fan_out(mod_all, md_s, md_r)
    spread(3)

    def project(q):
        def body(n):
            acc = contract(rows_b[...], w[q, :, :, lanes(n, 384)].reshape(D, 384), 1, 0)
            acc = acc.astype(BF).astype(F32)
            packed[rows8((q - 1) * D + n * 384, 384), :] = acc.T

        loop(3, body)

    complete(1)
    project(1)
    relay(2)
    complete(2)
    pass_on(mod_all, md_s, md_r)
    relay(3)
    project(2)
    attend(packed, bias, probs_t, None)
    complete(3)
    project(3)
    attend_back(packed, probs_t, cot, grad)
    grad_b[...] = grad[...].astype(BF)
    gt_all[:, lanes(s)] = grad_b[pl.ds(pl.multiple_of(s * 432, 16), 432), :]
    for k in range(1, NS):
        go(cols_copy(grad_b, gt_all, 432, gt_s, gt_r, k))

    def back_body(b):
        acc = jnp.zeros((576, T), F32)
        for q in range(1, CHUNKS):
            acc += contract(w[q, pl.ds(NY * b, NY)].reshape(576, D), grad_b[pl.ds((q - 1) * D, D), :], 1, 0)
        fp[rows8(b * 576, 576), :] = acc

    loop(NC, back_body)
    unpermute(fp, ft)
    t_to_rows(ft, rows_t, D)
    dx = rows_t[...] * sc[...]
    xh = xhat[...]
    m1 = jnp.mean(dx, axis=-1, keepdims=True)
    m2 = jnp.mean(dx * xh, axis=-1, keepdims=True)
    g_out[...] = (rstd[:, 0:1] * (dx - m1 - xh * m2)).astype(BF)
    g_in[own, :] = g_out[own, :]
    for k in range(1, NS):
        go(rows_copy(g_out, g_in, g_s, g_r, k))
    for k in range(1, NS):
        rows_copy(g_out, g_in, g_s, g_r, k).wait_recv()

    def tok_body(j):
        gt_b[rows8(j * 128, 128), :] = g_in[:, lanes(j)].astype(F32).T.astype(BF)

    loop(9, tok_body)
    g_all[:, lanes(s)] = gt_b[pl.ds(pl.multiple_of(s * 144, 16), 144), :]
    for k in range(1, NS):
        go(cols_copy(gt_b, g_all, 144, gc_s, gc_r, k))

    def mixed_body(b):
        fp[rows8(b * 576, 576), :] = contract(
            w[0, pl.ds(NY * b, NY)].reshape(576, D), gt_b[...], 1, 0
        )

    loop(NC, mixed_body)
    unpermute(fp, ft)

    fanned(mod_all, md_s, md_r)
    for k in range(1, NS):
        cols_copy(grad_b, gt_all, 432, gt_s, gt_r, k).wait_recv()

    def gwi_body(b):
        gwi_p[b] = contract(mod_all[rows8(b * 288, 288), :], gt_all[...], 1, 1).astype(BF)

    loop(NY, gwi_body)
    go(sum_c(gwi_p, gwi_c, ri_s, ri_r))
    fanned(mixed_all, mx_s, mx_r)
    for k in range(1, NS):
        cols_copy(gt_b, g_all, 144, gc_s, gc_r, k).wait_recv()

    def gwo_body(b):
        gwo_p[b] = contract(mixed_all[rows8(b * 288, 288), :], g_all[...], 1, 1).astype(BF)

    loop(NY, gwo_body)
    go(sum_c(gwo_p, gwo_c, ro_s, ro_r))
    add_c(gwi_p, gwi_c, gwi_h, gwi_y, ri_s, ri_r)
    add_c(gwo_p, gwo_c, gwo_h, gwo_y, ro_s, ro_r)

    def out_body(j):
        out_tok[:, lanes(j)] = ungroup(g_in[:, lanes(j)].astype(F32)).astype(BF)

    loop(9, out_body)
    attend_back(spat, probs, ft, grad, 0, 12)
    add_y(gwi_h, gwi_y, gwi_t, gwi_z, ri_s, ri_r)
    add_y(gwo_h, gwo_y, gwo_t, gwo_z, ro_s, ro_r)
    attend_back(spat, probs, ft, grad, 12, 4)

    def qkv_body(j):
        out_qkv[:, lanes(j)] = ungroup(grad[rows8(j * 128, 128), :].T).astype(BF)

    loop(27, qkv_body)
    add_z(gwi_t, gwi_z, ri_s, ri_r, out_gwi)
    add_z(gwo_t, gwo_z, ro_s, ro_r, out_gwo)
    for cp in started:
        cp.wait_send()


def time_modulation(timesteps):
    half = D // 2
    frequency = jnp.exp(-math.log(10000.0) * jnp.arange(half, dtype=F32) / half)
    angles = timesteps.astype(F32)[:, None] * frequency[None, :]
    cosine, sine = jnp.cos(angles), jnp.sin(angles)
    return (
        1.0 + 0.5 * jnp.concatenate([cosine, sine], axis=-1),
        0.5 * jnp.concatenate([sine, cosine], axis=-1),
    )


def shards(qkv_spatial, tokens, timesteps, w_out, w_in, grad_out):
    sc, sh = time_modulation(timesteps)
    tail = jnp.concatenate([w_out[MAIN:], w_in[MAIN:]], axis=1)
    tail = tail.reshape(TAIL, 36, 128).transpose(1, 0, 2).reshape(144, 128)
    dma = lambda *n: DMA(n)
    scratch = [
        VMEM((CHUNKS, NY * NC, BLOCK, D), BF),
        VMEM((NZ, 144, 128), BF),
        VMEM((3 * D, T), F32),
        VMEM((3 * D, T), F32),
        VMEM((HEADS, T, T), F32),
        VMEM((HEADS, T, T), F32),
        VMEM((T, T), F32),
        VMEM((3 * D, T), F32),
        VMEM((3 * D, T), BF),
        VMEM((D, T), F32),
        VMEM((D, T), F32),
        VMEM((T, D), BF),
        VMEM((T, D), F32),
        VMEM((T, D), BF),
        VMEM((T, D), BF),
        VMEM((T, D), BF),
        VMEM((T, D), F32),
        VMEM((T, 128), F32),
        VMEM((D, NS * T), BF),
        VMEM((D, NS * T), BF),
        VMEM((432, NS * T), BF),
        VMEM((144, NS * T), BF),
        VMEM((D, T), F32),
        VMEM((T, D), BF),
        VMEM((D, T), BF),
        *[VMEM(n + (m,), BF) for m in (432, 144)
          for n in ((NY, 288), (NY, 144), (NY, 144), (3, 144), (4, 48), (4, 48))],
        dma(4, 3), dma(4, 3), dma(3), dma(3), dma(4, 4), dma(4, 4), dma(4, 4), dma(4, 4),
        dma(5), dma(5), dma(5), dma(5),
        dma(7), dma(7), dma(7), dma(7), dma(7), dma(7), dma(7), dma(7),
        dma(8), dma(8), dma(8), dma(8),
    ]
    spec = pl.BlockSpec(memory_space=VMEM)
    gq, gt, gwo, gwi = pl.pallas_call(
        kernel,
        out_shape=(
            jax.ShapeDtypeStruct((T, 3 * D), BF),
            jax.ShapeDtypeStruct((T, D), BF),
            jax.ShapeDtypeStruct((SHARD, 144), F32),
            jax.ShapeDtypeStruct((SHARD, 432), F32),
        ),
        in_specs=[spec] * 8,
        out_specs=(spec,) * 4,
        scratch_shapes=scratch,
        compiler_params=pltpu.CompilerParams(
            collective_id=0, has_side_effects=True, vmem_limit_bytes=60 * 1024 * 1024
        ),
    )(
        qkv_spatial.reshape(T, 3 * D), tokens.reshape(T, D), grad_out.reshape(T, D),
        w_out, w_in, tail, sc, sh,
    )
    return gq.reshape(qkv_spatial.shape), gt.reshape(tokens.shape), gwo, gwi


def solution(mesh):
    placed = (
        P("dp", "seq", None, None),
        P("dp", "seq", None, None),
        P("dp"),
        P("dp", None),
        P("dp", None),
        P("dp", None, "seq", None),
    )
    return jax.shard_map(
        shards,
        mesh=mesh,
        in_specs=placed,
        out_specs=(
            P("dp", "seq", None, None),
            P("dp", "seq", None, None),
            P("dp", "seq"),
            P("dp", "seq"),
        ),
        check_vma=False,
    )
```

```python
import functools
import math

import jax
import jax.numpy as jnp
from jax import lax
from jax.experimental import pallas as pl
from jax.experimental.pallas import tpu as pltpu
from jax.sharding import PartitionSpec as P

HEADS = 16
D = 1152
HEAD = D // HEADS
T = 128
NY, NZ, NC, NS = 4, 4, 2, 8
NX = 4
SHARD = 36
MAIN, TAIL = 32, 4
BLOCK = NZ * SHARD
UNIT = 384
FIRST = (0, 3, 10, 6)
COUNT = (3, 3, 2, 4)
SHARED = 3
F32, BF = jnp.float32, jnp.bfloat16
MESH = pl.DeviceIdType.MESH
SCALE = 1.0 / math.sqrt(HEAD)
VMEM = pltpu.VMEM
DMA = pltpu.SemaphoreType.DMA


def contract(a, b, da, db):
    return lax.dot_general(a, b, (((da,), (db,)), ((), ())), preferred_element_type=F32)


def regroup(block):
    return jnp.concatenate(
        [block[64 * f + 8 * p : 64 * f + 8 * p + 8] for p in range(8) for f in range(2)], axis=0
    )


def ungroup(block):
    return jnp.concatenate(
        [block[16 * p + 8 * f : 16 * p + 8 * f + 8] for f in range(2) for p in range(8)], axis=0
    )


def lanes(i, n=128):
    return pl.ds(pl.multiple_of(i * n, 128), n)


def rows8(start, n):
    return pl.ds(pl.multiple_of(start, 8), n)


def loop(n, body, unroll=1):
    lax.fori_loop(0, n, lambda i, c: (body(i), c)[1], 0, unroll=unroll)


def rows_to_t(src, dst, n, group=False):
    def body(j):
        x = src[:, lanes(j)].astype(F32)
        if group:
            x = regroup(x)
        dst[rows8(j * 128, 128), :] = x.T.astype(dst.dtype)

    loop(n // 128, body)


def t_to_rows(src, dst, n):
    def body(j):
        dst[:, lanes(j)] = src[rows8(j * 128, 128), :].T.astype(dst.dtype)

    loop(n // 128, body)


def permute(src, dst):
    def body(y):
        x = src[rows8(y * 288, 288), :]
        for c in range(NC):
            parts = [x[72 * z + 36 * c : 72 * z + 36 * c + 32] for z in range(NZ)]
            parts += [x[72 * z + 36 * c + 32 : 72 * z + 36 * c + 36] for z in range(NZ)]
            dst[rows8(576 * c + y * 144, 144), :] = jnp.concatenate(parts, axis=0)

    loop(NY, body)


def unpermute(src, dst):
    def body(y):
        x = [src[rows8(576 * c + y * 144, 144), :] for c in range(NC)]
        parts = []
        for z in range(NZ):
            for c in range(NC):
                parts.append(x[c][32 * z : 32 * z + 32])
                parts.append(x[c][128 + 4 * z : 128 + 4 * z + 4])
        dst[rows8(y * 288, 288), :] = jnp.concatenate(parts, axis=0)

    loop(NY, body)


def head_slices(ref, h):
    return [ref[rows8(D * i + HEAD * h, HEAD), :].astype(BF) for i in range(3)]


def attend(packed, bias, probs, out):
    def body(h):
        for hh in (2 * h, 2 * h + 1):
            q = packed[rows8(HEAD * hh, HEAD), :].astype(BF)
            k = packed[rows8(D + HEAD * hh, HEAD), :].astype(BF)
            s = contract(k, q, 0, 0) * SCALE + bias[...]
            e = jnp.exp(s - jnp.max(s, axis=0, keepdims=True))
            p = e / jnp.sum(e, axis=0, keepdims=True)
            probs[hh] = p
            if out is not None:
                v = packed[rows8(2 * D + HEAD * hh, HEAD), :].astype(BF)
                o = contract(v, p.astype(BF), 1, 0)
                out[rows8(HEAD * hh, HEAD), :] = o.astype(BF).astype(F32)

    loop(HEADS // 2, body)


def attend_back(packed, probs, cot, grad, first=0, count=HEADS):
    def body(h):
        h = h + first // 2
        for hh in (2 * h, 2 * h + 1):
            q, k, v = head_slices(packed, hh)
            do = cot[rows8(HEAD * hh, HEAD), :].astype(BF)
            p = probs[hh]
            dp = contract(v, do, 0, 0).astype(BF).astype(F32)
            dv = contract(do, p.astype(BF), 1, 1)
            ds = p * (dp - jnp.sum(dp * p, axis=0, keepdims=True)) * SCALE
            ds = ds.astype(BF)
            dq = contract(k, ds, 1, 0)
            dk = contract(q, ds, 1, 1)
            grad[rows8(HEAD * hh, HEAD), :] = dq
            grad[rows8(D + HEAD * hh, HEAD), :] = dk
            grad[rows8(2 * D + HEAD * hh, HEAD), :] = dv

    loop(count // 2, body)


def kernel(
    qkv, tokens, gout, wo, wi, tail, sc, sh,
    out_qkv, out_tok, out_gwo, out_gwi,
    w, tails, packed, spat, probs, probs_t, bias, grad, grad_b, ft, fp, rows_b, rows_t, hid, hid_in, g_out,
    xhat, rstd, mixed_all, mod_all, gt_all, g_all, cot, g_in, gt_b,
    gwi_p, gwi_c, gwi_h, gwi_y, gwi_t, gwi_z, gwo_p, gwo_c, gwo_h, gwo_y, gwo_t, gwo_z,
    z_s, z_r, t_s, t_r, y_s, y_r, x_s, x_r, c_s, c_r, mx_s, mx_r, md_s, md_r,
    h_s, h_r, g_s, g_r, gt_s, gt_r, gc_s, gc_r, ri_s, ri_r, ro_s, ro_r,
):
    d = lax.axis_index("dp")
    s = lax.axis_index("seq")
    y, u = d // 8, d % 8
    z, c = u // 2, u % 2
    x, zl = s // 2, s % 2

    def z_peer(k):
        return (y * 8 + lax.rem(z + k, NZ) * 2 + c, s)

    def y_peer(k):
        return (lax.rem(y + k, NY) * 8 + u, s)

    core_peer = (d + 1 - 2 * c, s)

    def u_peer(k):
        return (y * 8 + lax.rem(u + k, 8), s)

    def x_peer(k):
        return (d, lax.rem(x + k, NX) * 2 + zl)

    pair = (d, s + 1 - 2 * zl)

    def s_peer(k):
        return (d, lax.rem(s + k, NS))

    peers = (
        [z_peer(k) for k in range(1, NZ)]
        + [y_peer(k) for k in range(1, NY)]
        + [u_peer(k) for k in range(1, 8)]
        + [s_peer(k) for k in range(1, NS)]
    )
    peers = peers[3:]
    barrier = pltpu.get_barrier_semaphore()
    for p in peers:
        pl.semaphore_signal(barrier, inc=1, device_id=p, device_id_type=MESH)

    started = []

    def copy(src, dst, ss, rs, to):
        return pltpu.make_async_remote_copy(
            src_ref=src, dst_ref=dst, send_sem=ss, recv_sem=rs, device_id=to, device_id_type=MESH
        )

    def go(cp):
        cp.start()
        started.append(cp)

    def units(q):
        if q == SHARED:
            return pl.ds(FIRST[q] + x, 1)
        return pl.ds(FIRST[q], COUNT[q])

    main_rows = pl.ds(pl.multiple_of(z * MAIN, 16), MAIN)

    def z_copy(q, k):
        part = w.at[units(q), c, y, main_rows, :]
        return copy(part, part, z_s.at[q, k - 1], z_r.at[q, k - 1], z_peer(k))

    def t_copy(k):
        return copy(tail, tails.at[z], t_s.at[k - 1], t_r.at[k - 1], z_peer(k))

    def at_y(k):
        return lax.rem(y + NY + k, NY)

    def at_x(k):
        return FIRST[SHARED] + lax.rem(x + NX + k, NX)

    def y_copy(q, i):
        part = w.at[units(q), c, y]
        if i == 2:
            part = w.at[units(q), c, at_y(-1), pl.ds(0, 80), :]
        if i == 3:
            part = w.at[units(q), c, at_y(1), pl.ds(80, 64), :]
        return copy(part, part, y_s.at[q, i], y_r.at[q, i], y_peer(1 if i % 2 == 0 else 3))

    def x_copy(i):
        if i < 2:
            part = w.at[at_x(0), c]
        else:
            part = w.at[at_x(-1 if i == 2 else 1), c, pl.ds(2 * (i - 2), 2)]
        return copy(part, part, x_s.at[i], x_r.at[i], x_peer(1 if i % 2 == 0 else 3))

    def c_copy(q, i):
        step = (0, -1, 1, 2)[i]
        part = w.at[at_x(step), c] if q == SHARED else w.at[units(q), c, at_y(step)]
        return copy(part, part, c_s.at[q, i], c_r.at[q, i], core_peer)

    def gather_copy(buf, ss, rs, i):
        if i == 0:
            part, to = buf.at[:, lanes(s)], pair
        elif i < 3:
            part, to = buf.at[:, lanes(x, 256)], x_peer(1 if i == 1 else 3)
        elif i == 3:
            part, to = buf.at[:, lanes(2 * lax.rem(x + 3, NX))], x_peer(1)
        else:
            part, to = buf.at[:, lanes(2 * lax.rem(x + 1, NX) + 1)], x_peer(3)
        return copy(part, part, ss.at[i], rs.at[i], to)

    def rows_copy(src, dst, ss, rs, k):
        to = lax.rem(s + k, NS)
        return copy(
            src.at[pl.ds(pl.multiple_of(to * 16, 16), 16), :],
            dst.at[pl.ds(pl.multiple_of(s * 16, 16), 16), :],
            ss.at[k - 1], rs.at[k - 1], s_peer(k),
        )

    def cols_copy(src, dst, n, ss, rs, k):
        to = lax.rem(s + k, NS)
        return copy(
            src.at[pl.ds(pl.multiple_of(to * n, 16), n), :], dst.at[:, lanes(s)],
            ss.at[k - 1], rs.at[k - 1], s_peer(k),
        )

    def sum_c(part, got, ss, rs):
        return copy(
            part.at[:, pl.ds(pl.multiple_of((1 - c) * 144, 16), 144), :], got, ss.at[0], rs.at[0], core_peer
        )

    def sum_y(half, got, ss, rs, k):
        return copy(half.at[lax.rem(y + k, NY)], got.at[k - 1], ss.at[k], rs.at[k], y_peer(k))

    def sum_z(slab, got, ss, rs, j):
        return copy(slab.at[j], got.at[z], ss.at[4 + j], rs.at[4 + z], (y * 8 + 4 * c + j, s))

    def add_c(part, got, half, ygot, ss, rs):
        sum_c(part, got, ss, rs).wait_recv()

        def body(b):
            own_half = part[b, pl.ds(pl.multiple_of(c * 144, 16), 144), :].astype(F32)
            half[b] = (own_half + got[b].astype(F32)).astype(BF)

        loop(NY, body)
        for k in range(1, NY):
            go(sum_y(half, ygot, ss, rs, k))

    def add_y(half, got, slab, zgot, ss, rs):
        for k in range(1, NY):
            sum_y(half, got, ss, rs, k).wait_recv()
        acc = half[y].astype(F32)
        for k in range(1, NY):
            acc += got[k - 1].astype(F32)
        for j in range(4):
            slab[j, 0:SHARD, :] = acc[SHARD * j : SHARD * j + SHARD].astype(BF)
            slab[j, SHARD:48, :] = jnp.zeros((48 - SHARD, acc.shape[1]), BF)
        for j in range(4):
            @pl.when(4 * c + j != u)
            def _():
                sum_z(slab, zgot, ss, rs, j).start()

            @pl.when(4 * c + j == u)
            def _():
                zgot[z] = slab[j]

    def add_z(slab, zgot, ss, rs, out):
        for zz in range(NZ):
            @pl.when((zz != z) | (u // 4 != c))
            def _():
                copy(slab.at[0], zgot.at[zz], ss.at[4], rs.at[4 + zz], core_peer).wait_recv()
        acc = zgot[0].astype(F32)
        for zz in range(1, NZ):
            acc += zgot[zz].astype(F32)
        out[...] = acc[0:SHARD]
        for j in range(4):
            @pl.when(4 * c + j != u)
            def _():
                sum_z(slab, zgot, ss, rs, j).wait_send()

    for n in range(3):
        w[n, c, y, main_rows, :] = wo[0:MAIN, n * UNIT : n * UNIT + UNIT]
    for n in (3, 4, 5, 10, 11):
        w[n, c, y, main_rows, :] = wi[0:MAIN, (n - 3) * UNIT : (n - 2) * UNIT]
    w[at_x(0), c, y, main_rows, :] = wi[0:MAIN, lanes(at_x(0) - 3, UNIT)]
    tails[z] = tail[...]
    pl.semaphore_wait(barrier, len(peers))

    for k in range(1, NZ):
        go(t_copy(k))
    for q in (SHARED, 0, 1, 2):
        for k in range(1, NZ):
            go(z_copy(q, k))

    rows_to_t(qkv, spat, 3 * D, group=True)

    for k in range(1, NZ):
        t_copy(k).wait_recv()

    low = lax.broadcasted_iota(jnp.int32, (8, 128), 0) < 4

    def tail_tiles(m):
        full = [tails[zz, pl.ds(pl.multiple_of(m * 16, 16), 16), :].astype(F32) for zz in range(NZ)]
        tiles = []
        for half in range(2):
            a = [v[8 * half : 8 * half + 8] for v in full]
            r = [pltpu.roll(v, 4, 0) for v in a]
            even = [jnp.where(low, a[0], r[1]), jnp.where(low, a[2], r[3])]
            odd = [jnp.where(low, r[0], a[1]), jnp.where(low, r[2], a[3])]
            tiles += [jnp.concatenate(t, axis=0).astype(BF) for t in (even, odd)]
        return tiles

    for m in range(9):
        for i, tile in enumerate(tail_tiles(m)):
            n, j = divmod(4 * m + i, 3)

            def put():
                w[n, c, y, pl.ds(NZ * MAIN, 16), pl.ds(128 * j, 128)] = tile

            if FIRST[SHARED] <= n < FIRST[SHARED] + NX:
                pl.when(x == n - FIRST[SHARED])(put)
            else:
                put()

    def spread(q):
        for k in range(1, NZ):
            z_copy(q, k).wait_recv()
        go(y_copy(q, 0))
        go(y_copy(q, 1))
        if q != SHARED:
            go(c_copy(q, 0))

    def relay(q):
        for i in range(2):
            y_copy(q, i).wait_recv()
            go(y_copy(q, 2 + i))
            if q != SHARED:
                go(c_copy(q, 1 + i))

    def complete(q):
        for i in range(2):
            y_copy(q, 2 + i).wait_recv()
        if q == SHARED:
            go(x_copy(0))
            go(x_copy(1))
            go(c_copy(q, 0))
        else:
            go(c_copy(q, 3))

    def x_relay():
        for i in range(2):
            x_copy(i).wait_recv()
            go(x_copy(2 + i))
            go(c_copy(SHARED, 1 + i))

    def x_complete():
        for i in range(2):
            x_copy(2 + i).wait_recv()
        go(c_copy(SHARED, 3))

    def both_cores(q):
        for i in range(4):
            c_copy(q, i).wait_recv()

    def fan_out(buf, ss, rs):
        gather_copy(buf, ss, rs, 0).wait_recv()
        for i in (1, 2):
            go(gather_copy(buf, ss, rs, i))

    def pass_on(buf, ss, rs):
        for i in (1, 2):
            gather_copy(buf, ss, rs, i).wait_recv()
            go(gather_copy(buf, ss, rs, 2 + i))

    def fanned(buf, ss, rs):
        for i in (3, 4):
            gather_copy(buf, ss, rs, i).wait_recv()

    def weight(n):
        return w[n].reshape(D, UNIT)

    spread(SHARED)

    ki = lax.broadcasted_iota(jnp.int32, (T, T), 0)
    qi = lax.broadcasted_iota(jnp.int32, (T, T), 1)
    bias[...] = jnp.where((ki // 8) % 2 == (qi // 8) % 2, 0.0, -1e30).astype(F32)
    attend(spat, bias, probs, ft)
    spread(0)
    relay(SHARED)
    mixed_all[:, lanes(s)] = ft[...].astype(BF)
    permute(ft, fp)
    t_to_rows(fp, rows_b, D)
    complete(SHARED)
    bias[...] = jnp.where(ki % 8 == qi % 8, 0.0, -1e30).astype(F32)
    rows_to_t(gout, cot, D)
    spread(1)
    relay(0)
    spread(2)
    x_relay()
    complete(0)
    go(gather_copy(mixed_all, mx_s, mx_r, 0))
    both_cores(0)

    def hidden_body(n):
        tok = regroup(tokens[:, lanes(n, 384)].astype(F32))
        acc = contract(rows_b[...], weight(n), 1, 0)
        hid[:, lanes(n, 384)] = (tok + acc).astype(BF)

    loop(3, hidden_body)
    own = pl.ds(pl.multiple_of(s * 16, 16), 16)
    hid_in[own, :] = hid[own, :]
    for k in range(1, NS):
        go(rows_copy(hid, hid_in, h_s, h_r, k))
    relay(1)
    x_complete()
    for k in range(1, NS):
        rows_copy(hid, hid_in, h_s, h_r, k).wait_recv()
    fan_out(mixed_all, mx_s, mx_r)

    hf = hid_in[...].astype(F32)
    centred = hf - jnp.mean(hf, axis=-1, keepdims=True)
    inv = lax.rsqrt(jnp.mean(centred * centred, axis=-1, keepdims=True) + 1e-06)
    xh = centred * inv
    xhat[...] = xh
    rstd[...] = jnp.broadcast_to(inv, (T, 128))
    rows_t[...] = (xh * sc[...] + sh[...]).astype(BF).astype(F32)
    rows_to_t(rows_t, ft, D)
    mod_all[:, lanes(s)] = ft[...].astype(BF)
    go(gather_copy(mod_all, md_s, md_r, 0))
    permute(ft, fp)
    t_to_rows(fp, rows_b, D)
    complete(1)
    relay(2)
    fan_out(mod_all, md_s, md_r)

    def project(first, count):
        def body(i):
            acc = contract(rows_b[...], weight(first + i), 1, 0)
            packed[rows8((first - 3 + i) * UNIT, UNIT), :] = acc.astype(BF).astype(F32).T

        loop(count, body)

    both_cores(SHARED)
    project(6, 4)
    both_cores(1)
    project(3, 3)
    pass_on(mixed_all, mx_s, mx_r)
    complete(2)
    attend(packed, bias, probs_t, None)
    both_cores(2)
    project(10, 2)
    attend_back(packed, probs_t, cot, grad)
    grad_b[...] = grad[...].astype(BF)
    gt_all[:, lanes(s)] = grad_b[pl.ds(pl.multiple_of(s * 432, 16), 432), :]

    def weight_t(n, b):
        return jnp.concatenate([w[n + i, b].reshape(576, UNIT) for i in range(3)], axis=1)

    def back_body(b):
        acc = jnp.zeros((576, T), F32)
        for q in range(3):
            acc += contract(weight_t(3 + 3 * q, b), grad_b[pl.ds(q * D, D), :], 1, 0)
        fp[rows8(b * 576, 576), :] = acc

    loop(NC, back_body)
    unpermute(fp, ft)
    t_to_rows(ft, rows_t, D)
    dx = rows_t[...] * sc[...]
    xh = xhat[...]
    m1 = jnp.mean(dx, axis=-1, keepdims=True)
    m2 = jnp.mean(dx * xh, axis=-1, keepdims=True)
    g_out[...] = (rstd[:, 0:1] * (dx - m1 - xh * m2)).astype(BF)
    g_in[own, :] = g_out[own, :]
    for k in range(1, NS):
        go(rows_copy(g_out, g_in, g_s, g_r, k))
    for k in range(1, NS):
        go(cols_copy(grad_b, gt_all, 432, gt_s, gt_r, k))
    pass_on(mod_all, md_s, md_r)
    for k in range(1, NS):
        rows_copy(g_out, g_in, g_s, g_r, k).wait_recv()

    def tok_body(j):
        gt_b[rows8(j * 128, 128), :] = g_in[:, lanes(j)].astype(F32).T.astype(BF)

    loop(9, tok_body)
    g_all[:, lanes(s)] = gt_b[pl.ds(pl.multiple_of(s * 144, 16), 144), :]
    for k in range(1, NS):
        go(cols_copy(gt_b, g_all, 144, gc_s, gc_r, k))

    def mixed_body(b):
        fp[rows8(b * 576, 576), :] = contract(
            weight_t(0, b), gt_b[...], 1, 0
        )

    loop(NC, mixed_body)
    unpermute(fp, ft)

    attend_back(spat, probs, ft, grad)

    def out_body(j):
        out_tok[:, lanes(j)] = ungroup(g_in[:, lanes(j)].astype(F32)).astype(BF)

    loop(9, out_body)

    fanned(mod_all, md_s, md_r)
    for k in range(1, NS):
        cols_copy(grad_b, gt_all, 432, gt_s, gt_r, k).wait_recv()

    def gwi_body(b):
        gwi_p[b] = contract(mod_all[rows8(b * 288, 288), :], gt_all[...], 1, 1).astype(BF)

    loop(NY, gwi_body)
    go(sum_c(gwi_p, gwi_c, ri_s, ri_r))
    fanned(mixed_all, mx_s, mx_r)
    for k in range(1, NS):
        cols_copy(gt_b, g_all, 144, gc_s, gc_r, k).wait_recv()

    def gwo_body(b):
        gwo_p[b] = contract(mixed_all[rows8(b * 288, 288), :], g_all[...], 1, 1).astype(BF)

    loop(NY, gwo_body)
    go(sum_c(gwo_p, gwo_c, ro_s, ro_r))
    add_c(gwi_p, gwi_c, gwi_h, gwi_y, ri_s, ri_r)
    add_c(gwo_p, gwo_c, gwo_h, gwo_y, ro_s, ro_r)

    def qkv_body(j):
        out_qkv[:, lanes(j)] = ungroup(grad[rows8(j * 128, 128), :].T).astype(BF)

    loop(27, qkv_body)
    add_y(gwi_h, gwi_y, gwi_t, gwi_z, ri_s, ri_r)
    add_y(gwo_h, gwo_y, gwo_t, gwo_z, ro_s, ro_r)
    add_z(gwi_t, gwi_z, ri_s, ri_r, out_gwi)
    add_z(gwo_t, gwo_z, ro_s, ro_r, out_gwo)
    for cp in started:
        cp.wait_send()


def time_modulation(timesteps):
    half = D // 2
    frequency = jnp.exp(-math.log(10000.0) * jnp.arange(half, dtype=F32) / half)
    angles = timesteps.astype(F32)[:, None] * frequency[None, :]
    cosine, sine = jnp.cos(angles), jnp.sin(angles)
    return (
        1.0 + 0.5 * jnp.concatenate([cosine, sine], axis=-1),
        0.5 * jnp.concatenate([sine, cosine], axis=-1),
    )


def shards(qkv_spatial, tokens, timesteps, w_out, w_in, grad_out):
    sc, sh = time_modulation(timesteps)
    tail = jnp.concatenate([w_out[MAIN:], w_in[MAIN:]], axis=1)
    tail = tail.reshape(TAIL, 36, 128).transpose(1, 0, 2).reshape(144, 128)
    dma = lambda *n: DMA(n)
    scratch = [
        VMEM((12, NC, NY, BLOCK, UNIT), BF),
        VMEM((NZ, 144, 128), BF),
        VMEM((3 * D, T), F32),
        VMEM((3 * D, T), F32),
        VMEM((HEADS, T, T), F32),
        VMEM((HEADS, T, T), F32),
        VMEM((T, T), F32),
        VMEM((3 * D, T), F32),
        VMEM((3 * D, T), BF),
        VMEM((D, T), F32),
        VMEM((D, T), F32),
        VMEM((T, D), BF),
        VMEM((T, D), F32),
        VMEM((T, D), BF),
        VMEM((T, D), BF),
        VMEM((T, D), BF),
        VMEM((T, D), F32),
        VMEM((T, 128), F32),
        VMEM((D, NS * T), BF),
        VMEM((D, NS * T), BF),
        VMEM((432, NS * T), BF),
        VMEM((144, NS * T), BF),
        VMEM((D, T), F32),
        VMEM((T, D), BF),
        VMEM((D, T), BF),
        *[VMEM(n + (m,), BF) for m in (432, 144)
          for n in ((NY, 288), (NY, 144), (NY, 144), (3, 144), (4, 48), (4, 48))],
        dma(4, 3), dma(4, 3), dma(3), dma(3), dma(4, 4), dma(4, 4), dma(4), dma(4), dma(4, 4), dma(4, 4),
        dma(5), dma(5), dma(5), dma(5),
        dma(7), dma(7), dma(7), dma(7), dma(7), dma(7), dma(7), dma(7),
        dma(8), dma(8), dma(8), dma(8),
    ]
    spec = pl.BlockSpec(memory_space=VMEM)
    gq, gt, gwo, gwi = pl.pallas_call(
        kernel,
        out_shape=(
            jax.ShapeDtypeStruct((T, 3 * D), BF),
            jax.ShapeDtypeStruct((T, D), BF),
            jax.ShapeDtypeStruct((SHARD, 144), F32),
            jax.ShapeDtypeStruct((SHARD, 432), F32),
        ),
        in_specs=[spec] * 8,
        out_specs=(spec,) * 4,
        scratch_shapes=scratch,
        compiler_params=pltpu.CompilerParams(
            collective_id=0, has_side_effects=True, vmem_limit_bytes=60 * 1024 * 1024
        ),
    )(
        qkv_spatial.reshape(T, 3 * D), tokens.reshape(T, D), grad_out.reshape(T, D),
        w_out, w_in, tail, sc, sh,
    )
    return gq.reshape(qkv_spatial.shape), gt.reshape(tokens.shape), gwo, gwi


def solution(mesh):
    placed = (
        P("dp", "seq", None, None),
        P("dp", "seq", None, None),
        P("dp"),
        P("dp", None),
        P("dp", None),
        P("dp", None, "seq", None),
    )
    return jax.shard_map(
        shards,
        mesh=mesh,
        in_specs=placed,
        out_specs=(
            P("dp", "seq", None, None),
            P("dp", "seq", None, None),
            P("dp", "seq"),
            P("dp", "seq"),
        ),
        check_vma=False,
    )
```

```python
import functools
import math

import jax
import jax.numpy as jnp
from jax import lax
from jax.experimental import pallas as pl
from jax.experimental.pallas import tpu as pltpu
from jax.sharding import PartitionSpec as P

HEADS = 16
D = 1152
HEAD = D // HEADS
GROUP = 4
T = 128
NY, NZ, NC, NS = 4, 4, 2, 8
NX = 4
SHARD = 36
MAIN, TAIL = 32, 4
BLOCK = NZ * SHARD
TILE = 128
FIRST = (0, 17, 27, 9)
COUNT = (9, 10, 9, 8)
SHARED = 3
PER_X = 2
F32, BF = jnp.float32, jnp.bfloat16
MESH = pl.DeviceIdType.MESH
SCALE = 1.0 / math.sqrt(HEAD)
VMEM = pltpu.VMEM
DMA = pltpu.SemaphoreType.DMA


def contract(a, b, da, db):
    return lax.dot_general(a, b, (((da,), (db,)), ((), ())), preferred_element_type=F32)


def regroup(block):
    return jnp.concatenate(
        [block[64 * f + 8 * p : 64 * f + 8 * p + 8] for p in range(8) for f in range(2)], axis=0
    )


def ungroup(block):
    return jnp.concatenate(
        [block[16 * p + 8 * f : 16 * p + 8 * f + 8] for f in range(2) for p in range(8)], axis=0
    )


def lanes(i, n=128):
    return pl.ds(pl.multiple_of(i * n, 128), n)


def rows8(start, n):
    return pl.ds(pl.multiple_of(start, 8), n)


def loop(n, body, unroll=1):
    lax.fori_loop(0, n, lambda i, c: (body(i), c)[1], 0, unroll=unroll)


def rows_to_t(src, dst, n, group=False):
    def body(j):
        x = src[:, lanes(j)].astype(F32)
        if group:
            x = regroup(x)
        dst[rows8(j * 128, 128), :] = x.T.astype(dst.dtype)

    loop(n // 128, body)


def t_to_rows(src, dst, n):
    def body(j):
        dst[:, lanes(j)] = src[rows8(j * 128, 128), :].T.astype(dst.dtype)

    loop(n // 128, body)


def permute(src, dst):
    def body(y):
        x = src[rows8(y * 288, 288), :]
        for c in range(NC):
            parts = [x[72 * z + 36 * c : 72 * z + 36 * c + 32] for z in range(NZ)]
            parts += [x[72 * z + 36 * c + 32 : 72 * z + 36 * c + 36] for z in range(NZ)]
            dst[rows8(576 * c + y * 144, 144), :] = jnp.concatenate(parts, axis=0)

    loop(NY, body)


def unpermute(src, dst):
    def body(y):
        x = [src[rows8(576 * c + y * 144, 144), :] for c in range(NC)]
        parts = []
        for z in range(NZ):
            for c in range(NC):
                parts.append(x[c][32 * z : 32 * z + 32])
                parts.append(x[c][128 + 4 * z : 128 + 4 * z + 4])
        dst[rows8(y * 288, 288), :] = jnp.concatenate(parts, axis=0)

    loop(NY, body)


def head_slices(ref, h):
    return [ref[rows8(D * i + HEAD * h, HEAD), :].astype(BF) for i in range(3)]


def attend(packed, bias, probs, out):
    def body(h):
        for hh in [GROUP * h + i for i in range(GROUP)]:
            q = packed[rows8(HEAD * hh, HEAD), :].astype(BF)
            k = packed[rows8(D + HEAD * hh, HEAD), :].astype(BF)
            s = contract(k, q, 0, 0) * SCALE + bias[...]
            e = jnp.exp(s - jnp.max(s, axis=0, keepdims=True))
            p = e / jnp.sum(e, axis=0, keepdims=True)
            probs[hh] = p
            if out is not None:
                v = packed[rows8(2 * D + HEAD * hh, HEAD), :].astype(BF)
                o = contract(v, p.astype(BF), 1, 0)
                out[rows8(HEAD * hh, HEAD), :] = o.astype(BF).astype(F32)

    loop(HEADS // GROUP, body)


def attend_back(packed, probs, cot, grad, first=0, count=HEADS):
    def body(h):
        h = h + first // GROUP
        for hh in [GROUP * h + i for i in range(GROUP)]:
            q, k, v = head_slices(packed, hh)
            do = cot[rows8(HEAD * hh, HEAD), :].astype(BF)
            p = probs[hh]
            dp = contract(v, do, 0, 0).astype(BF).astype(F32)
            dv = contract(do, p.astype(BF), 1, 1)
            ds = p * (dp - jnp.sum(dp * p, axis=0, keepdims=True)) * SCALE
            ds = ds.astype(BF)
            dq = contract(k, ds, 1, 0)
            dk = contract(q, ds, 1, 1)
            grad[rows8(HEAD * hh, HEAD), :] = dq
            grad[rows8(D + HEAD * hh, HEAD), :] = dk
            grad[rows8(2 * D + HEAD * hh, HEAD), :] = dv

    loop(count // GROUP, body)


def kernel(
    qkv_h, tokens_h, gout_h, wo_h, wi_h, sc, sh,
    out_qkv, out_tok, out_gwo, out_gwi,
    qkv, tokens, gout, wo, wi, tail, w, tails, packed, spat, probs, probs_t, bias, grad, grad_b, ft, fp, rows_b, rows_t, hid, hid_in, g_out,
    xhat, rstd, mixed_all, mod_all, gt_all, g_all, cot, g_in, gt_b,
    gwi_p, gwi_c, gwi_h, gwi_y, gwi_t, gwi_z, gwo_p, gwo_c, gwo_h, gwo_y, gwo_t, gwo_z,
    in_s, z_s, z_r, t_s, t_r, y_s, y_r, x_s, x_r, c_s, c_r, mx_s, mx_r, md_s, md_r,
    h_s, h_r, g_s, g_r, gt_s, gt_r, gc_s, gc_r, ri_s, ri_r, ro_s, ro_r,
):
    d = lax.axis_index("dp")
    s = lax.axis_index("seq")
    y, u = d // 8, d % 8
    z, c = u // 2, u % 2
    x, zl = s // 2, s % 2

    def z_peer(k):
        return (y * 8 + lax.rem(z + k, NZ) * 2 + c, s)

    def y_peer(k):
        return (lax.rem(y + k, NY) * 8 + u, s)

    core_peer = (d + 1 - 2 * c, s)

    def u_peer(k):
        return (y * 8 + lax.rem(u + k, 8), s)

    def x_peer(k):
        return (d, lax.rem(x + k, NX) * 2 + zl)

    pair = (d, s + 1 - 2 * zl)

    def s_peer(k):
        return (d, lax.rem(s + k, NS))

    peers = (
        [z_peer(k) for k in range(1, NZ)]
        + [y_peer(k) for k in range(1, NY)]
        + [u_peer(k) for k in range(1, 8)]
        + [s_peer(k) for k in range(1, NS)]
    )
    peers = peers[3:]
    loads = [
        pltpu.make_async_copy(a, b, in_s.at[i])
        for i, (a, b) in enumerate(
            ((wi_h, wi), (wo_h, wo), (qkv_h, qkv), (gout_h, gout), (tokens_h, tokens))
        )
    ]
    for cp in loads:
        cp.start()
    barrier = pltpu.get_barrier_semaphore()
    for p in peers:
        pl.semaphore_signal(barrier, inc=1, device_id=p, device_id_type=MESH)

    started = []

    def copy(src, dst, ss, rs, to):
        return pltpu.make_async_remote_copy(
            src_ref=src, dst_ref=dst, send_sem=ss, recv_sem=rs, device_id=to, device_id_type=MESH
        )

    def go(cp):
        cp.start()
        started.append(cp)

    def at_x(k):
        return FIRST[SHARED] + PER_X * lax.rem(x + NX + k, NX)

    def units(q):
        if q == SHARED:
            return pl.ds(at_x(0), PER_X)
        return pl.ds(FIRST[q], COUNT[q])

    main_rows = pl.ds(pl.multiple_of(z * MAIN, 16), MAIN)

    def z_copy(q, k):
        part = w.at[units(q), c, y, main_rows, :]
        return copy(part, part, z_s.at[q, k - 1], z_r.at[q, k - 1], z_peer(k))

    def t_copy(k):
        return copy(tail, tails.at[z], t_s.at[k - 1], t_r.at[k - 1], z_peer(k))

    def at_y(k):
        return lax.rem(y + NY + k, NY)

    def y_copy(q, i):
        part = w.at[units(q), c, y]
        if i == 2:
            part = w.at[units(q), c, at_y(-1), pl.ds(0, 80), :]
        if i == 3:
            part = w.at[units(q), c, at_y(1), pl.ds(80, 64), :]
        return copy(part, part, y_s.at[q, i], y_r.at[q, i], y_peer(1 if i % 2 == 0 else 3))

    def x_copy(i):
        if i < 2:
            part = w.at[units(SHARED), c]
        else:
            part = w.at[pl.ds(at_x(-1 if i == 2 else 1), PER_X), c, pl.ds(2 * (i - 2), 2)]
        return copy(part, part, x_s.at[i], x_r.at[i], x_peer(1 if i % 2 == 0 else 3))

    def c_copy(q, i):
        step = (0, -1, 1, 2)[i]
        part = w.at[pl.ds(at_x(step), PER_X), c] if q == SHARED else w.at[units(q), c, at_y(step)]
        return copy(part, part, c_s.at[q, i], c_r.at[q, i], core_peer)

    other = s + 1 - 2 * zl

    def gather_copy(buf, ss, rs, i):
        slot = (s, s, s, other, other, 2 * lax.rem(x + 3, NX) + zl, 2 * lax.rem(x + 1, NX) + 1 - zl)[i]
        to = pair if i == 0 else x_peer(1 if i % 2 == 1 else 3)
        part = buf.at[:, lanes(slot)]
        return copy(part, part, ss.at[i], rs.at[i], to)

    def rows_copy(src, dst, ss, rs, k):
        to = lax.rem(s + k, NS)
        return copy(
            src.at[pl.ds(pl.multiple_of(to * 16, 16), 16), :],
            dst.at[pl.ds(pl.multiple_of(s * 16, 16), 16), :],
            ss.at[k - 1], rs.at[k - 1], s_peer(k),
        )

    def cols_copy(src, dst, n, ss, rs, k):
        to = lax.rem(s + k, NS)
        return copy(
            src.at[pl.ds(pl.multiple_of(to * n, 16), n), :], dst.at[:, lanes(s)],
            ss.at[k - 1], rs.at[k - 1], s_peer(k),
        )

    def sum_c(part, got, ss, rs):
        return copy(
            part.at[:, pl.ds(pl.multiple_of((1 - c) * 144, 16), 144), :], got, ss.at[0], rs.at[0], core_peer
        )

    def sum_y(half, got, ss, rs, k):
        return copy(half.at[lax.rem(y + k, NY)], got.at[k - 1], ss.at[k], rs.at[k], y_peer(k))

    def sum_z(slab, got, ss, rs, j):
        return copy(slab.at[j], got.at[z], ss.at[4 + j], rs.at[4 + z], (y * 8 + 4 * c + j, s))

    def add_c(part, got, half, ygot, ss, rs):
        sum_c(part, got, ss, rs).wait_recv()

        def body(b):
            own_half = part[b, pl.ds(pl.multiple_of(c * 144, 16), 144), :].astype(F32)
            half[b] = (own_half + got[b].astype(F32)).astype(BF)

        loop(NY, body)
        for k in range(1, NY):
            go(sum_y(half, ygot, ss, rs, k))

    def add_y(half, got, slab, zgot, ss, rs):
        for k in range(1, NY):
            sum_y(half, got, ss, rs, k).wait_recv()
        acc = half[y].astype(F32)
        for k in range(1, NY):
            acc += got[k - 1].astype(F32)
        for j in range(4):
            slab[j, 0:SHARD, :] = acc[SHARD * j : SHARD * j + SHARD].astype(BF)
            slab[j, SHARD:48, :] = jnp.zeros((48 - SHARD, acc.shape[1]), BF)
        for j in range(4):
            @pl.when(4 * c + j != u)
            def _():
                sum_z(slab, zgot, ss, rs, j).start()

            @pl.when(4 * c + j == u)
            def _():
                zgot[z] = slab[j]

    def add_z(slab, zgot, ss, rs, out):
        for zz in range(NZ):
            @pl.when((zz != z) | (u // 4 != c))
            def _():
                copy(slab.at[0], zgot.at[zz], ss.at[4], rs.at[4 + zz], core_peer).wait_recv()
        acc = zgot[0].astype(F32)
        for zz in range(1, NZ):
            acc += zgot[zz].astype(F32)
        out[...] = acc[0:SHARD]
        for j in range(4):
            @pl.when(4 * c + j != u)
            def _():
                sum_z(slab, zgot, ss, rs, j).wait_send()

    for cp in loads[:2]:
        cp.wait()
    pieces = []
    for ref in (wo, wi):
        rows = ref[MAIN:SHARD, :].astype(F32)
        pieces += [rows[:, j * TILE : j * TILE + TILE] for j in range(rows.shape[1] // TILE)]
    tail[...] = jnp.concatenate(pieces, axis=0).astype(BF)
    for n in range(9):
        w[n, c, y, main_rows, :] = wo[0:MAIN, n * TILE : n * TILE + TILE]
    for n in range(17, 36):
        w[n, c, y, main_rows, :] = wi[0:MAIN, (n - 9) * TILE : (n - 8) * TILE]
    for i in range(PER_X):
        w[at_x(0) + i, c, y, main_rows, :] = wi[0:MAIN, lanes(at_x(0) + i - 9)]
    tails[z] = tail[...]
    loads[2].wait()
    rows_to_t(qkv, spat, 3 * D, group=True)
    pl.semaphore_wait(barrier, len(peers))

    for k in range(1, NZ):
        go(t_copy(k))

    def z_start(q):
        for k in range(1, NZ):
            go(z_copy(q, k))

    z_start(SHARED)
    z_start(0)

    for k in range(1, NZ):
        t_copy(k).wait_recv()

    low = lax.broadcasted_iota(jnp.int32, (8, 128), 0) < 4

    def tail_tiles(m):
        full = [tails[zz, pl.ds(pl.multiple_of(m * 16, 16), 16), :].astype(F32) for zz in range(NZ)]
        tiles = []
        for half in range(2):
            a = [v[8 * half : 8 * half + 8] for v in full]
            r = [pltpu.roll(v, 4, 0) for v in a]
            even = [jnp.where(low, a[0], r[1]), jnp.where(low, a[2], r[3])]
            odd = [jnp.where(low, r[0], a[1]), jnp.where(low, r[2], a[3])]
            tiles += [jnp.concatenate(t, axis=0).astype(BF) for t in (even, odd)]
        return tiles

    for m in range(9):
        for i, tile in enumerate(tail_tiles(m)):
            n = 4 * m + i

            def put(n=n, tile=tile):
                w[n, c, y, pl.ds(NZ * MAIN, 16), :] = tile

            if FIRST[SHARED] <= n < FIRST[SHARED] + COUNT[SHARED]:
                pl.when(x == (n - FIRST[SHARED]) // PER_X)(put)
            else:
                put()

    def spread(q):
        for k in range(1, NZ):
            z_copy(q, k).wait_recv()
        go(y_copy(q, 0))
        go(y_copy(q, 1))
        if q != SHARED:
            go(c_copy(q, 0))

    def relay(q):
        for i in range(2):
            y_copy(q, i).wait_recv()
            go(y_copy(q, 2 + i))
            if q != SHARED:
                go(c_copy(q, 1 + i))

    def complete(q):
        for i in range(2):
            y_copy(q, 2 + i).wait_recv()
        if q == SHARED:
            go(x_copy(0))
            go(x_copy(1))
            go(c_copy(q, 0))
        else:
            go(c_copy(q, 3))

    def x_relay():
        for i in range(2):
            x_copy(i).wait_recv()
            go(x_copy(2 + i))
            go(c_copy(SHARED, 1 + i))

    def x_complete():
        for i in range(2):
            x_copy(2 + i).wait_recv()
        go(c_copy(SHARED, 3))

    def both_cores(q):
        for i in range(4):
            c_copy(q, i).wait_recv()

    def fan_own(buf, ss, rs):
        for i in (0, 1, 2):
            go(gather_copy(buf, ss, rs, i))

    def fan_other(buf, ss, rs):
        gather_copy(buf, ss, rs, 0).wait_recv()
        for i in (3, 4):
            go(gather_copy(buf, ss, rs, i))

    def pass_own(buf, ss, rs):
        gather_copy(buf, ss, rs, 1).wait_recv()
        go(gather_copy(buf, ss, rs, 5))

    def pass_other(buf, ss, rs):
        gather_copy(buf, ss, rs, 4).wait_recv()
        go(gather_copy(buf, ss, rs, 6))

    def fanned(buf, ss, rs):
        for i in (2, 3, 5, 6):
            gather_copy(buf, ss, rs, i).wait_recv()

    def weight(n):
        return jnp.concatenate([w[n + i].reshape(D, TILE) for i in range(3)], axis=1)

    spread(SHARED)

    ki = lax.broadcasted_iota(jnp.int32, (T, T), 0)
    qi = lax.broadcasted_iota(jnp.int32, (T, T), 1)
    bias[...] = jnp.where((ki // 8) % 2 == (qi // 8) % 2, 0.0, -1e30).astype(F32)
    attend(spat, bias, probs, ft)
    mixed_all[:, lanes(s)] = ft[...].astype(BF)
    fan_own(mixed_all, mx_s, mx_r)
    z_start(1)
    z_start(2)
    relay(SHARED)
    spread(0)
    permute(ft, fp)
    t_to_rows(fp, rows_b, D)
    loads[3].wait()
    loads[4].wait()
    complete(SHARED)
    bias[...] = jnp.where(ki % 8 == qi % 8, 0.0, -1e30).astype(F32)
    rows_to_t(gout, cot, D)
    pass_own(mixed_all, mx_s, mx_r)
    relay(0)
    spread(1)
    x_relay()
    complete(0)
    both_cores(0)

    def hidden_body(n):
        tok = regroup(tokens[:, lanes(n, 384)].astype(F32))
        acc = contract(rows_b[...], weight(3 * n), 1, 0)
        hid[:, lanes(n, 384)] = (tok + acc).astype(BF)

    loop(3, hidden_body)
    own = pl.ds(pl.multiple_of(s * 16, 16), 16)
    hid_in[own, :] = hid[own, :]
    for k in range(1, NS):
        go(rows_copy(hid, hid_in, h_s, h_r, k))
    fan_other(mixed_all, mx_s, mx_r)
    spread(2)
    relay(1)
    x_complete()
    for k in range(1, NS):
        rows_copy(hid, hid_in, h_s, h_r, k).wait_recv()

    hf = hid_in[...].astype(F32)
    centred = hf - jnp.mean(hf, axis=-1, keepdims=True)
    inv = lax.rsqrt(jnp.mean(centred * centred, axis=-1, keepdims=True) + 1e-06)
    xh = centred * inv
    xhat[...] = xh
    rstd[...] = jnp.broadcast_to(inv, (T, 128))
    rows_t[...] = (xh * sc[...] + sh[...]).astype(BF).astype(F32)
    rows_to_t(rows_t, ft, D)
    mod_all[:, lanes(s)] = ft[...].astype(BF)
    fan_own(mod_all, md_s, md_r)
    permute(ft, fp)
    t_to_rows(fp, rows_b, D)

    def project(first, count):
        def body(i):
            acc = contract(rows_b[...], weight(first + 3 * i), 1, 0)
            packed[rows8((first - 9) * TILE + 3 * TILE * i, 3 * TILE), :] = acc.astype(BF).astype(F32).T

        loop(count, body)

    pass_other(mixed_all, mx_s, mx_r)
    complete(1)
    relay(2)
    both_cores(SHARED)
    project(9, 2)
    both_cores(1)
    project(15, 4)
    fan_other(mod_all, md_s, md_r)
    attend(packed, bias, probs_t, None)
    pass_own(mod_all, md_s, md_r)
    complete(2)
    both_cores(2)
    project(27, 3)
    attend_back(packed, probs_t, cot, grad)
    grad_b[...] = grad[...].astype(BF)
    pass_other(mod_all, md_s, md_r)
    gt_all[:, lanes(s)] = grad_b[pl.ds(pl.multiple_of(s * 432, 16), 432), :]

    def weight_t(n, b):
        return jnp.concatenate([w[n + i, b].reshape(576, TILE) for i in range(9)], axis=1)

    def back_body(b):
        acc = jnp.zeros((576, T), F32)
        for q in range(3):
            acc += contract(weight_t(9 + 9 * q, b), grad_b[pl.ds(q * D, D), :], 1, 0)
        fp[rows8(b * 576, 576), :] = acc

    loop(NC, back_body)
    unpermute(fp, ft)
    t_to_rows(ft, rows_t, D)
    dx = rows_t[...] * sc[...]
    xh = xhat[...]
    m1 = jnp.mean(dx, axis=-1, keepdims=True)
    m2 = jnp.mean(dx * xh, axis=-1, keepdims=True)
    g_out[...] = (rstd[:, 0:1] * (dx - m1 - xh * m2)).astype(BF)
    g_in[own, :] = g_out[own, :]
    for k in range(1, NS):
        go(rows_copy(g_out, g_in, g_s, g_r, k))
    for k in range(1, NS):
        go(cols_copy(grad_b, gt_all, 432, gt_s, gt_r, k))
    for k in range(1, NS):
        rows_copy(g_out, g_in, g_s, g_r, k).wait_recv()

    def tok_body(j):
        gt_b[rows8(j * 128, 128), :] = g_in[:, lanes(j)].astype(F32).T.astype(BF)

    loop(9, tok_body)
    g_all[:, lanes(s)] = gt_b[pl.ds(pl.multiple_of(s * 144, 16), 144), :]
    for k in range(1, NS):
        go(cols_copy(gt_b, g_all, 144, gc_s, gc_r, k))

    def mixed_body(b):
        fp[rows8(b * 576, 576), :] = contract(
            weight_t(0, b), gt_b[...], 1, 0
        )

    loop(NC, mixed_body)
    unpermute(fp, ft)

    attend_back(spat, probs, ft, grad, 0, 8)
    fanned(mod_all, md_s, md_r)
    for k in range(1, NS):
        cols_copy(grad_b, gt_all, 432, gt_s, gt_r, k).wait_recv()

    def gwi_body(b):
        gwi_p[b] = contract(mod_all[rows8(b * 288, 288), :], gt_all[...], 1, 1).astype(BF)

    loop(NY, gwi_body)
    go(sum_c(gwi_p, gwi_c, ri_s, ri_r))
    attend_back(spat, probs, ft, grad, 8, 8)
    add_c(gwi_p, gwi_c, gwi_h, gwi_y, ri_s, ri_r)
    fanned(mixed_all, mx_s, mx_r)
    for k in range(1, NS):
        cols_copy(gt_b, g_all, 144, gc_s, gc_r, k).wait_recv()

    def gwo_body(b):
        gwo_p[b] = contract(mixed_all[rows8(b * 288, 288), :], g_all[...], 1, 1).astype(BF)

    loop(NY, gwo_body)
    go(sum_c(gwo_p, gwo_c, ro_s, ro_r))

    def out_body(j):
        out_tok[:, lanes(j)] = ungroup(g_in[:, lanes(j)].astype(F32)).astype(BF)

    loop(9, out_body)
    add_c(gwo_p, gwo_c, gwo_h, gwo_y, ro_s, ro_r)

    def qkv_body(j):
        out_qkv[:, lanes(j)] = ungroup(grad[rows8(j * 128, 128), :].T).astype(BF)

    loop(27, qkv_body)
    add_y(gwi_h, gwi_y, gwi_t, gwi_z, ri_s, ri_r)
    add_y(gwo_h, gwo_y, gwo_t, gwo_z, ro_s, ro_r)
    add_z(gwi_t, gwi_z, ri_s, ri_r, out_gwi)
    add_z(gwo_t, gwo_z, ro_s, ro_r, out_gwo)
    for cp in started:
        cp.wait_send()


def hand_over(*refs):
    for src, dst in zip(refs[:4], refs[4:]):
        dst[...] = src[...]


def time_modulation(timesteps):
    half = D // 2
    frequency = jnp.exp(-math.log(10000.0) * jnp.arange(half, dtype=F32) / half)
    angles = timesteps.astype(F32)[:, None] * frequency[None, :]
    cosine, sine = jnp.cos(angles), jnp.sin(angles)
    return (
        1.0 + 0.5 * jnp.concatenate([cosine, sine], axis=-1),
        0.5 * jnp.concatenate([sine, cosine], axis=-1),
    )


def shards(qkv_spatial, tokens, timesteps, w_out, w_in, grad_out):
    sc, sh = time_modulation(timesteps)
    dma = lambda *n: DMA(n)
    scratch = [
        VMEM((T, 3 * D), BF), VMEM((T, D), BF), VMEM((T, D), BF),
        VMEM((SHARD, D), BF), VMEM((SHARD, 3 * D), BF), VMEM((144, 128), BF),
        VMEM((36, NC, NY, BLOCK, TILE), BF),
        VMEM((NZ, 144, 128), BF),
        VMEM((3 * D, T), F32),
        VMEM((3 * D, T), F32),
        VMEM((HEADS, T, T), F32),
        VMEM((HEADS, T, T), F32),
        VMEM((T, T), F32),
        VMEM((3 * D, T), F32),
        VMEM((3 * D, T), BF),
        VMEM((D, T), F32),
        VMEM((D, T), F32),
        VMEM((T, D), BF),
        VMEM((T, D), F32),
        VMEM((T, D), BF),
        VMEM((T, D), BF),
        VMEM((T, D), BF),
        VMEM((T, D), F32),
        VMEM((T, 128), F32),
        VMEM((D, NS * T), BF),
        VMEM((D, NS * T), BF),
        VMEM((432, NS * T), BF),
        VMEM((144, NS * T), BF),
        VMEM((D, T), F32),
        VMEM((T, D), BF),
        VMEM((D, T), BF),
        *[VMEM(n + (m,), BF) for m in (432, 144)
          for n in ((NY, 288), (NY, 144), (NY, 144), (3, 144), (4, 48), (4, 48))],
        dma(5), dma(4, 3), dma(4, 3), dma(3), dma(3), dma(4, 4), dma(4, 4), dma(4), dma(4), dma(4, 4), dma(4, 4),
        dma(7), dma(7), dma(7), dma(7),
        dma(7), dma(7), dma(7), dma(7), dma(7), dma(7), dma(7), dma(7),
        dma(8), dma(8), dma(8), dma(8),
    ]
    spec = pl.BlockSpec(memory_space=VMEM)
    results = pl.pallas_call(
        kernel,
        out_shape=(
            jax.ShapeDtypeStruct((T, 3 * D), BF),
            jax.ShapeDtypeStruct((T, D), BF),
            jax.ShapeDtypeStruct((SHARD, 144), F32),
            jax.ShapeDtypeStruct((SHARD, 432), F32),
        ),
        in_specs=[pl.BlockSpec(memory_space=pl.ANY)] * 5 + [spec] * 2,
        out_specs=(spec,) * 4,
        scratch_shapes=scratch,
        compiler_params=pltpu.CompilerParams(
            collective_id=0, has_side_effects=True, vmem_limit_bytes=60 * 1024 * 1024
        ),
    )(
        qkv_spatial.reshape(T, 3 * D), tokens.reshape(T, D), grad_out.reshape(T, D),
        w_out, w_in, sc, sh,
    )
    gq, gt, gwo, gwi = pl.pallas_call(
        hand_over,
        out_shape=tuple(jax.ShapeDtypeStruct(r.shape, r.dtype) for r in results),
        in_specs=[spec] * 4,
        out_specs=(spec,) * 4,
    )(*results)
    return gq.reshape(qkv_spatial.shape), gt.reshape(tokens.shape), gwo, gwi


def solution(mesh):
    placed = (
        P("dp", "seq", None, None),
        P("dp", "seq", None, None),
        P("dp"),
        P("dp", None),
        P("dp", None),
        P("dp", None, "seq", None),
    )
    return jax.shard_map(
        shards,
        mesh=mesh,
        in_specs=placed,
        out_specs=(
            P("dp", "seq", None, None),
            P("dp", "seq", None, None),
            P("dp", "seq"),
            P("dp", "seq"),
        ),
        check_vma=False,
    )
```

```python
import functools
import math

import jax
import jax.numpy as jnp
from jax import lax
from jax.experimental import pallas as pl
from jax.experimental.pallas import tpu as pltpu
from jax.sharding import PartitionSpec as P

HEADS = 16
D = 1152
HEAD = D // HEADS
GROUP = 4
T = 128
NY, NZ, NC, NS = 4, 4, 2, 8
NX = 4
SHARD = 36
MAIN, TAIL = 32, 4
BLOCK = NZ * SHARD
TILE = 128
FIRST = (0, 17, 27, 9)
COUNT = (9, 10, 9, 8)
SHARED = 3
PER_X = 2
F32, BF = jnp.float32, jnp.bfloat16
MESH = pl.DeviceIdType.MESH
SCALE = 1.0 / math.sqrt(HEAD)
VMEM = pltpu.VMEM
DMA = pltpu.SemaphoreType.DMA


def contract(a, b, da, db):
    return lax.dot_general(a, b, (((da,), (db,)), ((), ())), preferred_element_type=F32)


def regroup(block):
    return jnp.concatenate(
        [block[64 * f + 8 * p : 64 * f + 8 * p + 8] for p in range(8) for f in range(2)], axis=0
    )


def ungroup(block):
    return jnp.concatenate(
        [block[16 * p + 8 * f : 16 * p + 8 * f + 8] for f in range(2) for p in range(8)], axis=0
    )


def lanes(i, n=128):
    return pl.ds(pl.multiple_of(i * n, 128), n)


def rows8(start, n):
    return pl.ds(pl.multiple_of(start, 8), n)


def loop(n, body, unroll=1):
    lax.fori_loop(0, n, lambda i, c: (body(i), c)[1], 0, unroll=unroll)


def rows_to_t(src, dst, n, group=False):
    def body(j):
        x = src[:, lanes(j)].astype(F32)
        if group:
            x = regroup(x)
        dst[rows8(j * 128, 128), :] = x.T.astype(dst.dtype)

    loop(n // 128, body)


def t_to_rows(src, dst, n):
    def body(j):
        dst[:, lanes(j)] = src[rows8(j * 128, 128), :].T.astype(dst.dtype)

    loop(n // 128, body)


def permute(src, dst):
    def body(y):
        x = src[rows8(y * 288, 288), :]
        for c in range(NC):
            parts = [x[72 * z + 36 * c : 72 * z + 36 * c + 32] for z in range(NZ)]
            parts += [x[72 * z + 36 * c + 32 : 72 * z + 36 * c + 36] for z in range(NZ)]
            dst[rows8(576 * c + y * 144, 144), :] = jnp.concatenate(parts, axis=0)

    loop(NY, body)


def unpermute(src, dst):
    def body(y):
        x = [src[rows8(576 * c + y * 144, 144), :] for c in range(NC)]
        parts = []
        for z in range(NZ):
            for c in range(NC):
                parts.append(x[c][32 * z : 32 * z + 32])
                parts.append(x[c][128 + 4 * z : 128 + 4 * z + 4])
        dst[rows8(y * 288, 288), :] = jnp.concatenate(parts, axis=0)

    loop(NY, body)


def head_slices(ref, h):
    return [ref[rows8(D * i + HEAD * h, HEAD), :].astype(BF) for i in range(3)]


def attend(packed, bias, probs, out, first=0, count=HEADS):
    def body(h):
        h = h + first // GROUP
        for hh in [GROUP * h + i for i in range(GROUP)]:
            q = packed[rows8(HEAD * hh, HEAD), :].astype(BF)
            k = packed[rows8(D + HEAD * hh, HEAD), :].astype(BF)
            s = contract(k, q, 0, 0) * SCALE + bias[...]
            e = jnp.exp(s - jnp.max(s, axis=0, keepdims=True))
            p = e / jnp.sum(e, axis=0, keepdims=True)
            probs[hh] = p
            if out is not None:
                v = packed[rows8(2 * D + HEAD * hh, HEAD), :].astype(BF)
                o = contract(v, p.astype(BF), 1, 0)
                out[rows8(HEAD * hh, HEAD), :] = o.astype(BF).astype(F32)

    loop(count // GROUP, body)


def attend_back(packed, probs, cot, grad, first=0, count=HEADS):
    def body(h):
        h = h + first // GROUP
        for hh in [GROUP * h + i for i in range(GROUP)]:
            q, k, v = head_slices(packed, hh)
            do = cot[rows8(HEAD * hh, HEAD), :].astype(BF)
            p = probs[hh]
            dp = contract(v, do, 0, 0).astype(BF).astype(F32)
            dv = contract(do, p.astype(BF), 1, 1)
            ds = p * (dp - jnp.sum(dp * p, axis=0, keepdims=True)) * SCALE
            ds = ds.astype(BF)
            dq = contract(k, ds, 1, 0)
            dk = contract(q, ds, 1, 1)
            grad[rows8(HEAD * hh, HEAD), :] = dq
            grad[rows8(D + HEAD * hh, HEAD), :] = dk
            grad[rows8(2 * D + HEAD * hh, HEAD), :] = dv

    loop(count // GROUP, body)


def kernel(
    qkv_h, tokens_h, gout_h, wo_h, wi_h, sc, sh,
    out_qkv, out_tok, out_gwo, out_gwi,
    qkv, tokens, gout, wo, wi, tail, w, tails, packed, spat, probs, probs_t, bias, grad, grad_b, ft, fp, rows_b, rows_t, hid, hid_in, g_out,
    xhat, rstd, mixed_all, mod_all, gt_all, g_all, cot, g_in, gt_b, gp_b, swap,
    gwi_p, gwi_c, gwi_h, gwi_y, gwi_t, gwi_z, gwo_p, gwo_c, gwo_h, gwo_y, gwo_t, gwo_z,
    in_s, z_s, z_r, t_s, t_r, y_s, y_r, x_s, x_r, c_s, c_r, mx_s, mx_r, md_s, md_r,
    h_s, h_r, g_s, g_r, gt_s, gt_r, gc_s, gc_r, ri_s, ri_r, ro_s, ro_r,
):
    d = lax.axis_index("dp")
    s = lax.axis_index("seq")
    y, u = d // 8, d % 8
    z, c = u // 2, u % 2
    x, zl = s // 2, s % 2

    def z_peer(k):
        return (y * 8 + lax.rem(z + k, NZ) * 2 + c, s)

    def y_peer(k):
        return (lax.rem(y + k, NY) * 8 + u, s)

    core_peer = (d + 1 - 2 * c, s)

    def u_peer(k):
        return (y * 8 + lax.rem(u + k, 8), s)

    def x_peer(k):
        return (d, lax.rem(x + k, NX) * 2 + zl)

    pair = (d, s + 1 - 2 * zl)

    def s_peer(k):
        return (d, lax.rem(s + k, NS))

    peers = (
        [z_peer(k) for k in range(1, NZ)]
        + [y_peer(k) for k in range(1, NY)]
        + [u_peer(k) for k in range(1, 8)]
        + [s_peer(k) for k in range(1, NS)]
    )
    peers = peers[3:]
    loads = [
        pltpu.make_async_copy(a, b, in_s.at[i])
        for i, (a, b) in enumerate(
            ((wi_h, wi), (wo_h, wo), (qkv_h, qkv), (gout_h, gout), (tokens_h, tokens))
        )
    ]
    for cp in loads:
        cp.start()
    barrier = pltpu.get_barrier_semaphore()
    for p in peers:
        pl.semaphore_signal(barrier, inc=1, device_id=p, device_id_type=MESH)

    started = []

    def copy(src, dst, ss, rs, to):
        return pltpu.make_async_remote_copy(
            src_ref=src, dst_ref=dst, send_sem=ss, recv_sem=rs, device_id=to, device_id_type=MESH
        )

    def go(cp):
        cp.start()
        started.append(cp)

    def at_x(k):
        return FIRST[SHARED] + PER_X * lax.rem(x + NX + k, NX)

    def units(q):
        if q == SHARED:
            return pl.ds(at_x(0), PER_X)
        return pl.ds(FIRST[q], COUNT[q])

    main_rows = pl.ds(pl.multiple_of(z * MAIN, 16), MAIN)

    def z_copy(q, k):
        part = w.at[units(q), c, y, main_rows, :]
        return copy(part, part, z_s.at[q, k - 1], z_r.at[q, k - 1], z_peer(k))

    def t_copy(k):
        return copy(tail, tails.at[z], t_s.at[k - 1], t_r.at[k - 1], z_peer(k))

    def at_y(k):
        return lax.rem(y + NY + k, NY)

    def y_copy(q, i):
        part = w.at[units(q), c, y]
        if i == 2:
            part = w.at[units(q), c, at_y(-1), pl.ds(0, 80), :]
        if i == 3:
            part = w.at[units(q), c, at_y(1), pl.ds(80, 64), :]
        return copy(part, part, y_s.at[q, i], y_r.at[q, i], y_peer(1 if i % 2 == 0 else 3))

    def x_copy(i):
        if i < 2:
            part = w.at[units(SHARED), c]
        else:
            part = w.at[pl.ds(at_x(-1 if i == 2 else 1), PER_X), c, pl.ds(2 * (i - 2), 2)]
        return copy(part, part, x_s.at[i], x_r.at[i], x_peer(1 if i % 2 == 0 else 3))

    def c_copy(q, i):
        step = (0, -1, 1, 2)[i]
        part = w.at[pl.ds(at_x(step), PER_X), c] if q == SHARED else w.at[units(q), c, at_y(step)]
        return copy(part, part, c_s.at[q, i], c_r.at[q, i], core_peer)

    other = s + 1 - 2 * zl

    def gather_copy(buf, ss, rs, i):
        slot = s
        if i in (3, 4):
            slot = other
        if i == 5:
            slot = 2 * lax.rem(x + 3, NX) + zl
        if i == 6:
            slot = 2 * lax.rem(x + 1, NX) + 1 - zl
        rows = pl.ds(0, D)
        if i in (1, 2):
            rows = pl.ds(0, D // 2)
        if i in (7, 8):
            rows = pl.ds(D // 2, D // 2)
        to = pair if i == 0 else x_peer(1 if i % 2 == 1 else 3)
        part = buf.at[rows, lanes(slot)]
        return copy(part, part, ss.at[i], rs.at[i], to)

    def rows_copy(src, dst, ss, rs, k):
        to = lax.rem(s + k, NS)
        return copy(
            src.at[pl.ds(pl.multiple_of(to * 16, 16), 16), :],
            dst.at[pl.ds(pl.multiple_of(s * 16, 16), 16), :],
            ss.at[k - 1], rs.at[k - 1], s_peer(k),
        )

    def cols_copy(src, dst, n, ss, rs, k):
        to = lax.rem(s + k, NS)
        return copy(
            src.at[pl.ds(pl.multiple_of(to * n, 16), n), :], dst.at[:, lanes(s)],
            ss.at[k - 1], rs.at[k - 1], s_peer(k),
        )

    def sum_c(part, got, ss, rs):
        return copy(
            part.at[:, pl.ds(pl.multiple_of((1 - c) * 144, 16), 144), :], got, ss.at[0], rs.at[0], core_peer
        )

    def sum_y(half, got, ss, rs, k):
        return copy(half.at[lax.rem(y + k, NY)], got.at[k - 1], ss.at[k], rs.at[k], y_peer(k))

    def sum_z(slab, got, ss, rs, j):
        return copy(slab.at[j], got.at[z], ss.at[4 + j], rs.at[4 + z], (y * 8 + 4 * c + j, s))

    def add_c(part, got, half, ygot, ss, rs):
        sum_c(part, got, ss, rs).wait_recv()

        def body(b):
            own_half = part[b, pl.ds(pl.multiple_of(c * 144, 16), 144), :].astype(F32)
            half[b] = (own_half + got[b].astype(F32)).astype(BF)

        loop(NY, body)
        for k in range(1, NY):
            go(sum_y(half, ygot, ss, rs, k))

    def add_y(half, got, slab, zgot, ss, rs):
        for k in range(1, NY):
            sum_y(half, got, ss, rs, k).wait_recv()
        acc = half[y].astype(F32)
        for k in range(1, NY):
            acc += got[k - 1].astype(F32)
        for j in range(4):
            slab[j, 0:SHARD, :] = acc[SHARD * j : SHARD * j + SHARD].astype(BF)
            slab[j, SHARD:48, :] = jnp.zeros((48 - SHARD, acc.shape[1]), BF)
        for j in range(4):
            @pl.when(4 * c + j != u)
            def _():
                sum_z(slab, zgot, ss, rs, j).start()

            @pl.when(4 * c + j == u)
            def _():
                zgot[z] = slab[j]

    def add_z(slab, zgot, ss, rs, out):
        for zz in range(NZ):
            @pl.when((zz != z) | (u // 4 != c))
            def _():
                copy(slab.at[0], zgot.at[zz], ss.at[4], rs.at[4 + zz], core_peer).wait_recv()
        acc = zgot[0].astype(F32)
        for zz in range(1, NZ):
            acc += zgot[zz].astype(F32)
        out[...] = acc[0:SHARD]
        for j in range(4):
            @pl.when(4 * c + j != u)
            def _():
                sum_z(slab, zgot, ss, rs, j).wait_send()

    for cp in loads[:2]:
        cp.wait()
    pieces = []
    for ref in (wo, wi):
        rows = ref[MAIN:SHARD, :].astype(F32)
        pieces += [rows[:, j * TILE : j * TILE + TILE] for j in range(rows.shape[1] // TILE)]
    tail[...] = jnp.concatenate(pieces, axis=0).astype(BF)
    for n in range(9):
        w[n, c, y, main_rows, :] = wo[0:MAIN, n * TILE : n * TILE + TILE]
    for n in range(17, 36):
        w[n, c, y, main_rows, :] = wi[0:MAIN, (n - 9) * TILE : (n - 8) * TILE]
    for i in range(PER_X):
        w[at_x(0) + i, c, y, main_rows, :] = wi[0:MAIN, lanes(at_x(0) + i - 9)]
    tails[z] = tail[...]
    loads[2].wait()
    rows_to_t(qkv, spat, 3 * D, group=True)
    pl.semaphore_wait(barrier, len(peers))

    for k in range(1, NZ):
        go(t_copy(k))

    def z_start(q):
        for k in range(1, NZ):
            go(z_copy(q, k))

    z_start(SHARED)
    z_start(0)

    ki = lax.broadcasted_iota(jnp.int32, (T, T), 0)
    qi = lax.broadcasted_iota(jnp.int32, (T, T), 1)
    bias[...] = jnp.where((ki // 8) % 2 == (qi // 8) % 2, 0.0, -1e30).astype(F32)

    def half_attention(i):
        half = pl.ds(i * (D // 2), D // 2)
        attend(spat, bias, probs, ft, 8 * i, 8)
        mixed_all[half, lanes(s)] = ft[half, :].astype(BF)
        for j in (1, 2):
            go(gather_copy(mixed_all, mx_s, mx_r, j + 6 * i))

    half_attention(0)

    for k in range(1, NZ):
        t_copy(k).wait_recv()

    low = lax.broadcasted_iota(jnp.int32, (8, 128), 0) < 4

    def tail_tiles(m):
        full = [tails[zz, pl.ds(pl.multiple_of(m * 16, 16), 16), :].astype(F32) for zz in range(NZ)]
        tiles = []
        for half in range(2):
            a = [v[8 * half : 8 * half + 8] for v in full]
            r = [pltpu.roll(v, 4, 0) for v in a]
            even = [jnp.where(low, a[0], r[1]), jnp.where(low, a[2], r[3])]
            odd = [jnp.where(low, r[0], a[1]), jnp.where(low, r[2], a[3])]
            tiles += [jnp.concatenate(t, axis=0).astype(BF) for t in (even, odd)]
        return tiles

    for m in range(9):
        for i, tile in enumerate(tail_tiles(m)):
            n = 4 * m + i

            def put(n=n, tile=tile):
                w[n, c, y, pl.ds(NZ * MAIN, 16), :] = tile

            if FIRST[SHARED] <= n < FIRST[SHARED] + COUNT[SHARED]:
                pl.when(x == (n - FIRST[SHARED]) // PER_X)(put)
            else:
                put()

    def spread(q):
        for k in range(1, NZ):
            z_copy(q, k).wait_recv()
        go(y_copy(q, 0))
        go(y_copy(q, 1))
        if q != SHARED:
            go(c_copy(q, 0))

    def relay(q):
        for i in range(2):
            y_copy(q, i).wait_recv()
            go(y_copy(q, 2 + i))
            if q != SHARED:
                go(c_copy(q, 1 + i))

    def complete(q):
        for i in range(2):
            y_copy(q, 2 + i).wait_recv()
        if q == SHARED:
            go(x_copy(0))
            go(x_copy(1))
            go(c_copy(q, 0))
        else:
            go(c_copy(q, 3))

    def x_relay():
        for i in range(2):
            x_copy(i).wait_recv()
            go(x_copy(2 + i))
            go(c_copy(SHARED, 1 + i))

    def x_complete():
        for i in range(2):
            x_copy(2 + i).wait_recv()
        go(c_copy(SHARED, 3))

    def both_cores(q):
        for i in range(4):
            c_copy(q, i).wait_recv()

    def fan_own(buf, ss, rs):
        for i in (0, 1, 2, 7, 8):
            go(gather_copy(buf, ss, rs, i))

    def fan_other(buf, ss, rs):
        gather_copy(buf, ss, rs, 0).wait_recv()
        for i in (3, 4):
            go(gather_copy(buf, ss, rs, i))

    def pass_own(buf, ss, rs):
        for i in (1, 7):
            gather_copy(buf, ss, rs, i).wait_recv()
        go(gather_copy(buf, ss, rs, 5))

    def pass_other(buf, ss, rs):
        gather_copy(buf, ss, rs, 4).wait_recv()
        go(gather_copy(buf, ss, rs, 6))

    def fanned(buf, ss, rs):
        for i in (2, 8, 3, 5, 6):
            gather_copy(buf, ss, rs, i).wait_recv()

    def weight(n):
        return jnp.concatenate([w[n + i].reshape(D, TILE) for i in range(3)], axis=1)

    spread(SHARED)

    half_attention(1)
    z_start(1)
    z_start(2)
    go(gather_copy(mixed_all, mx_s, mx_r, 0))
    relay(SHARED)
    spread(0)
    permute(ft, fp)
    t_to_rows(fp, rows_b, D)
    loads[3].wait()
    loads[4].wait()
    complete(SHARED)
    bias[...] = jnp.where(ki % 8 == qi % 8, 0.0, -1e30).astype(F32)
    rows_to_t(gout, cot, D)
    pass_own(mixed_all, mx_s, mx_r)

    def swap_body(i):
        row = lax.broadcasted_iota(jnp.int32, (T, NS * T), 0) + i * T
        col = lax.broadcasted_iota(jnp.int32, (T, NS * T), 1)
        want = (((col >> 4) & 7) << 7) | ((col >> 7) << 4) | (col & 15)
        swap[rows8(i * T, T), :] = jnp.where(row == want, 1.0, 0.0).astype(BF)

    loop(NS, swap_body)
    relay(0)
    spread(1)
    x_relay()
    complete(0)
    both_cores(0)

    def hidden_body(n):
        tok = regroup(tokens[:, lanes(n, 384)].astype(F32))
        acc = contract(rows_b[...], weight(3 * n), 1, 0)
        hid[:, lanes(n, 384)] = (tok + acc).astype(BF)

    loop(3, hidden_body)
    own = pl.ds(pl.multiple_of(s * 16, 16), 16)
    hid_in[own, :] = hid[own, :]
    for k in range(1, NS):
        go(rows_copy(hid, hid_in, h_s, h_r, k))
    fan_other(mixed_all, mx_s, mx_r)
    spread(2)
    relay(1)
    x_complete()
    for k in range(1, NS):
        rows_copy(hid, hid_in, h_s, h_r, k).wait_recv()

    hf = hid_in[...].astype(F32)
    centred = hf - jnp.mean(hf, axis=-1, keepdims=True)
    inv = lax.rsqrt(jnp.mean(centred * centred, axis=-1, keepdims=True) + 1e-06)
    xh = centred * inv
    xhat[...] = xh
    rstd[...] = jnp.broadcast_to(inv, (T, 128))
    rows_t[...] = (xh * sc[...] + sh[...]).astype(BF).astype(F32)
    rows_to_t(rows_t, ft, D)
    mod_all[:, lanes(s)] = ft[...].astype(BF)
    fan_own(mod_all, md_s, md_r)
    permute(ft, fp)
    t_to_rows(fp, rows_b, D)

    def project(first, count):
        def body(i):
            acc = contract(rows_b[...], weight(first + 3 * i), 1, 0)
            packed[rows8((first - 9) * TILE + 3 * TILE * i, 3 * TILE), :] = acc.astype(BF).astype(F32).T

        loop(count, body)

    complete(1)
    relay(2)
    both_cores(SHARED)
    project(9, 2)
    both_cores(1)
    project(15, 4)
    fan_other(mod_all, md_s, md_r)
    attend(packed, bias, probs_t, None)
    pass_own(mod_all, md_s, md_r)
    complete(2)
    both_cores(2)
    project(27, 3)
    pass_other(mod_all, md_s, md_r)
    attend_back(packed, probs_t, cot, grad)
    grad_b[...] = grad[...].astype(BF)
    gt_all[:, lanes(s)] = grad_b[pl.ds(pl.multiple_of(s * 432, 16), 432), :]
    for k in range(1, NS):
        go(cols_copy(grad_b, gt_all, 432, gt_s, gt_r, k))

    def weight_t(n, b):
        return jnp.concatenate([w[n + i, b].reshape(576, TILE) for i in range(9)], axis=1)

    def back_body(b):
        acc = jnp.zeros((576, T), F32)
        for q in range(3):
            acc += contract(weight_t(9 + 9 * q, b), grad_b[pl.ds(q * D, D), :], 1, 0)
        fp[rows8(b * 576, 576), :] = acc

    loop(NC, back_body)
    unpermute(fp, ft)
    t_to_rows(ft, rows_t, D)
    dx = rows_t[...] * sc[...]
    xh = xhat[...]
    m1 = jnp.mean(dx, axis=-1, keepdims=True)
    m2 = jnp.mean(dx * xh, axis=-1, keepdims=True)
    g_out[...] = (rstd[:, 0:1] * (dx - m1 - xh * m2)).astype(BF)
    g_in[own, :] = g_out[own, :]
    for k in range(1, NS):
        go(rows_copy(g_out, g_in, g_s, g_r, k))
    pass_other(mixed_all, mx_s, mx_r)
    rows_to_t(g_out, gp_b, D)
    g_all[:, lanes(s)] = gp_b[pl.ds(pl.multiple_of(s * 144, 16), 144), :]
    for k in range(1, NS):
        go(cols_copy(gp_b, g_all, 144, gc_s, gc_r, k))

    fanned(mod_all, md_s, md_r)
    for k in range(1, NS):
        cols_copy(grad_b, gt_all, 432, gt_s, gt_r, k).wait_recv()

    def gwi_body(b):
        gwi_p[b] = contract(mod_all[rows8(b * 288, 288), :], gt_all[...], 1, 1).astype(BF)

    loop(NY, gwi_body)
    go(sum_c(gwi_p, gwi_c, ri_s, ri_r))

    for k in range(1, NS):
        rows_copy(g_out, g_in, g_s, g_r, k).wait_recv()
    rows_to_t(g_in, gt_b, D)

    def mixed_body(b):
        fp[rows8(b * 576, 576), :] = contract(weight_t(0, b), gt_b[...], 1, 0)

    loop(NC, mixed_body)
    unpermute(fp, ft)
    add_c(gwi_p, gwi_c, gwi_h, gwi_y, ri_s, ri_r)

    fanned(mixed_all, mx_s, mx_r)
    for k in range(1, NS):
        cols_copy(gp_b, g_all, 144, gc_s, gc_r, k).wait_recv()
    g_sorted = contract(g_all[...], swap[...], 1, 0).astype(BF)
    g_all[...] = g_sorted

    def gwo_body(b):
        gwo_p[b] = contract(mixed_all[rows8(b * 288, 288), :], g_all[...], 1, 1).astype(BF)

    loop(NY, gwo_body)
    go(sum_c(gwo_p, gwo_c, ro_s, ro_r))
    attend_back(spat, probs, ft, grad, 0, 8)
    add_c(gwo_p, gwo_c, gwo_h, gwo_y, ro_s, ro_r)
    attend_back(spat, probs, ft, grad, 8, 8)
    add_y(gwi_h, gwi_y, gwi_t, gwi_z, ri_s, ri_r)

    def qkv_body(j):
        out_qkv[:, lanes(j)] = ungroup(grad[rows8(j * 128, 128), :].T).astype(BF)

    loop(27, qkv_body)
    add_y(gwo_h, gwo_y, gwo_t, gwo_z, ro_s, ro_r)

    def out_body(j):
        out_tok[:, lanes(j)] = ungroup(g_in[:, lanes(j)].astype(F32)).astype(BF)

    loop(9, out_body)
    add_z(gwi_t, gwi_z, ri_s, ri_r, out_gwi)
    add_z(gwo_t, gwo_z, ro_s, ro_r, out_gwo)
    for cp in started:
        cp.wait_send()


def hand_over(*refs):
    for src, dst in zip(refs[:4], refs[4:]):
        dst[...] = src[...]


def time_modulation(timesteps):
    half = D // 2
    frequency = jnp.exp(-math.log(10000.0) * jnp.arange(half, dtype=F32) / half)
    angles = timesteps.astype(F32)[:, None] * frequency[None, :]
    cosine, sine = jnp.cos(angles), jnp.sin(angles)
    return (
        1.0 + 0.5 * jnp.concatenate([cosine, sine], axis=-1),
        0.5 * jnp.concatenate([sine, cosine], axis=-1),
    )


def shards(qkv_spatial, tokens, timesteps, w_out, w_in, grad_out):
    sc, sh = time_modulation(timesteps)
    dma = lambda *n: DMA(n)
    scratch = [
        VMEM((T, 3 * D), BF), VMEM((T, D), BF), VMEM((T, D), BF),
        VMEM((SHARD, D), BF), VMEM((SHARD, 3 * D), BF), VMEM((144, 128), BF),
        VMEM((36, NC, NY, BLOCK, TILE), BF),
        VMEM((NZ, 144, 128), BF),
        VMEM((3 * D, T), F32),
        VMEM((3 * D, T), F32),
        VMEM((HEADS, T, T), F32),
        VMEM((HEADS, T, T), F32),
        VMEM((T, T), F32),
        VMEM((3 * D, T), F32),
        VMEM((3 * D, T), BF),
        VMEM((D, T), F32),
        VMEM((D, T), F32),
        VMEM((T, D), BF),
        VMEM((T, D), F32),
        VMEM((T, D), BF),
        VMEM((T, D), BF),
        VMEM((T, D), BF),
        VMEM((T, D), F32),
        VMEM((T, 128), F32),
        VMEM((D, NS * T), BF),
        VMEM((D, NS * T), BF),
        VMEM((432, NS * T), BF),
        VMEM((144, NS * T), BF),
        VMEM((D, T), F32),
        VMEM((T, D), BF),
        VMEM((D, T), BF),
        VMEM((D, T), BF),
        VMEM((NS * T, NS * T), BF),
        *[VMEM(n + (m,), BF) for m in (432, 144)
          for n in ((NY, 288), (NY, 144), (NY, 144), (3, 144), (4, 48), (4, 48))],
        dma(5), dma(4, 3), dma(4, 3), dma(3), dma(3), dma(4, 4), dma(4, 4), dma(4), dma(4), dma(4, 4), dma(4, 4),
        dma(9), dma(9), dma(9), dma(9),
        dma(7), dma(7), dma(7), dma(7), dma(7), dma(7), dma(7), dma(7),
        dma(8), dma(8), dma(8), dma(8),
    ]
    spec = pl.BlockSpec(memory_space=VMEM)
    results = pl.pallas_call(
        kernel,
        out_shape=(
            jax.ShapeDtypeStruct((T, 3 * D), BF),
            jax.ShapeDtypeStruct((T, D), BF),
            jax.ShapeDtypeStruct((SHARD, 144), F32),
            jax.ShapeDtypeStruct((SHARD, 432), F32),
        ),
        in_specs=[pl.BlockSpec(memory_space=pl.ANY)] * 5 + [spec] * 2,
        out_specs=(spec,) * 4,
        scratch_shapes=scratch,
        compiler_params=pltpu.CompilerParams(
            collective_id=0, has_side_effects=True, vmem_limit_bytes=60 * 1024 * 1024
        ),
    )(
        qkv_spatial.reshape(T, 3 * D), tokens.reshape(T, D), grad_out.reshape(T, D),
        w_out, w_in, sc, sh,
    )
    gq, gt, gwo, gwi = pl.pallas_call(
        hand_over,
        out_shape=tuple(jax.ShapeDtypeStruct(r.shape, r.dtype) for r in results),
        in_specs=[spec] * 4,
        out_specs=(spec,) * 4,
    )(*results)
    return gq.reshape(qkv_spatial.shape), gt.reshape(tokens.shape), gwo, gwi


def solution(mesh):
    placed = (
        P("dp", "seq", None, None),
        P("dp", "seq", None, None),
        P("dp"),
        P("dp", None),
        P("dp", None),
        P("dp", None, "seq", None),
    )
    return jax.shard_map(
        shards,
        mesh=mesh,
        in_specs=placed,
        out_specs=(
            P("dp", "seq", None, None),
            P("dp", "seq", None, None),
            P("dp", "seq"),
            P("dp", "seq"),
        ),
        check_vma=False,
    )
```

```python
import functools
import math

import jax
import jax.numpy as jnp
from jax import lax
from jax.experimental import pallas as pl
from jax.experimental.pallas import tpu as pltpu
from jax.sharding import PartitionSpec as P

HEADS = 16
D = 1152
HEAD = D // HEADS
GROUP = 8
T = 128
NY, NZ, NC, NS = 4, 4, 2, 8
NX = 4
SHARD = 36
MAIN, TAIL = 32, 4
BLOCK = NZ * SHARD
TILE = 128
FIRST = (0, 17, 27, 9)
COUNT = (9, 10, 9, 8)
SHARED = 3
PER_X = 2
F32, BF = jnp.float32, jnp.bfloat16
MESH = pl.DeviceIdType.MESH
SCALE = 1.0 / math.sqrt(HEAD)
VMEM = pltpu.VMEM
DMA = pltpu.SemaphoreType.DMA


def contract(a, b, da, db):
    return lax.dot_general(a, b, (((da,), (db,)), ((), ())), preferred_element_type=F32)


def regroup(block):
    return jnp.concatenate(
        [block[64 * f + 8 * p : 64 * f + 8 * p + 8] for p in range(8) for f in range(2)], axis=0
    )


def ungroup(block):
    return jnp.concatenate(
        [block[16 * p + 8 * f : 16 * p + 8 * f + 8] for f in range(2) for p in range(8)], axis=0
    )


def lanes(i, n=128):
    return pl.ds(pl.multiple_of(i * n, 128), n)


def rows8(start, n):
    return pl.ds(pl.multiple_of(start, 8), n)


def loop(n, body, unroll=1):
    lax.fori_loop(0, n, lambda i, c: (body(i), c)[1], 0, unroll=unroll)


def rows_to_t(src, dst, n, group=False):
    def body(j):
        x = src[:, lanes(j)].astype(F32)
        if group:
            x = regroup(x)
        dst[rows8(j * 128, 128), :] = x.T.astype(dst.dtype)

    loop(n // 128, body)


def t_to_rows(src, dst, n):
    def body(j):
        dst[:, lanes(j)] = src[rows8(j * 128, 128), :].T.astype(dst.dtype)

    loop(n // 128, body)


def permute(src, dst):
    def body(y):
        x = src[rows8(y * 288, 288), :]
        for c in range(NC):
            parts = [x[72 * z + 36 * c : 72 * z + 36 * c + 32] for z in range(NZ)]
            parts += [x[72 * z + 36 * c + 32 : 72 * z + 36 * c + 36] for z in range(NZ)]
            dst[rows8(576 * c + y * 144, 144), :] = jnp.concatenate(parts, axis=0)

    loop(NY, body)


def unpermute(src, dst):
    def body(y):
        x = [src[rows8(576 * c + y * 144, 144), :] for c in range(NC)]
        parts = []
        for z in range(NZ):
            for c in range(NC):
                parts.append(x[c][32 * z : 32 * z + 32])
                parts.append(x[c][128 + 4 * z : 128 + 4 * z + 4])
        dst[rows8(y * 288, 288), :] = jnp.concatenate(parts, axis=0)

    loop(NY, body)


def head_slices(ref, h):
    return [ref[rows8(D * i + HEAD * h, HEAD), :].astype(BF) for i in range(3)]


def attend(packed, bias, probs, out, first=0, count=HEADS):
    def body(h):
        h = h + first // GROUP
        for hh in [GROUP * h + i for i in range(GROUP)]:
            q = packed[rows8(HEAD * hh, HEAD), :].astype(BF)
            k = packed[rows8(D + HEAD * hh, HEAD), :].astype(BF)
            s = contract(k, q, 0, 0) * SCALE + bias[...]
            e = jnp.exp(s - jnp.max(s, axis=0, keepdims=True))
            p = e / jnp.sum(e, axis=0, keepdims=True)
            probs[hh] = p
            if out is not None:
                v = packed[rows8(2 * D + HEAD * hh, HEAD), :].astype(BF)
                o = contract(v, p.astype(BF), 1, 0)
                out[rows8(HEAD * hh, HEAD), :] = o.astype(BF).astype(F32)

    loop(count // GROUP, body)


def attend_back(packed, probs, cot, grad, first=0, count=HEADS):
    def body(h):
        h = h + first // GROUP
        for hh in [GROUP * h + i for i in range(GROUP)]:
            q, k, v = head_slices(packed, hh)
            do = cot[rows8(HEAD * hh, HEAD), :].astype(BF)
            p = probs[hh]
            dp = contract(v, do, 0, 0).astype(BF).astype(F32)
            dv = contract(do, p.astype(BF), 1, 1)
            ds = p * (dp - jnp.sum(dp * p, axis=0, keepdims=True)) * SCALE
            ds = ds.astype(BF)
            dq = contract(k, ds, 1, 0)
            dk = contract(q, ds, 1, 1)
            grad[rows8(HEAD * hh, HEAD), :] = dq
            grad[rows8(D + HEAD * hh, HEAD), :] = dk
            grad[rows8(2 * D + HEAD * hh, HEAD), :] = dv

    loop(count // GROUP, body)


def kernel(
    qkv_h, tokens_h, gout_h, wo_h, wi_h, sc, sh,
    out_qkv, out_tok, out_gwo, out_gwi,
    qkv, tokens, gout, wo, wi, tail, w, tails, packed, spat, probs, probs_t, bias, grad, grad_b, ft, fp, rows_b, rows_t, hid, hid_in, g_out,
    xhat, rstd, mixed_all, mod_all, gt_all, g_all, cot, g_in, gt_b, gp_b, swap,
    gwa_p, gwa_c, gwa_h, gwa_y, gwa_t, gwa_z, gwb_p, gwb_c, gwb_h, gwb_y, gwb_t, gwb_z, gwo_p, gwo_c, gwo_h, gwo_y, gwo_t, gwo_z,
    in_s, z_s, z_r, t_s, t_r, y_s, y_r, x_s, x_r, c_s, c_r, mx_s, mx_r, md_s, md_r,
    h_s, h_r, g_s, g_r, gt_s, gt_r, gc_s, gc_r, ra_s, ra_r, rb_s, rb_r, ro_s, ro_r,
):
    d = lax.axis_index("dp")
    s = lax.axis_index("seq")
    y, u = d // 8, d % 8
    z, c = u // 2, u % 2
    x, zl = s // 2, s % 2

    def z_peer(k):
        return (y * 8 + lax.rem(z + k, NZ) * 2 + c, s)

    def y_peer(k):
        return (lax.rem(y + k, NY) * 8 + u, s)

    core_peer = (d + 1 - 2 * c, s)

    def u_peer(k):
        return (y * 8 + lax.rem(u + k, 8), s)

    def x_peer(k):
        return (d, lax.rem(x + k, NX) * 2 + zl)

    pair = (d, s + 1 - 2 * zl)

    def s_peer(k):
        return (d, lax.rem(s + k, NS))

    peers = (
        [z_peer(k) for k in range(1, NZ)]
        + [y_peer(k) for k in range(1, NY)]
        + [u_peer(k) for k in range(1, 8)]
        + [s_peer(k) for k in range(1, NS)]
    )
    peers = peers[3:]
    loads = [
        pltpu.make_async_copy(a, b, in_s.at[i])
        for i, (a, b) in enumerate(
            ((wi_h, wi), (wo_h, wo), (qkv_h, qkv), (gout_h, gout), (tokens_h, tokens))
        )
    ]
    for cp in loads:
        cp.start()
    barrier = pltpu.get_barrier_semaphore()
    for p in peers:
        pl.semaphore_signal(barrier, inc=1, device_id=p, device_id_type=MESH)

    started = []

    def copy(src, dst, ss, rs, to):
        return pltpu.make_async_remote_copy(
            src_ref=src, dst_ref=dst, send_sem=ss, recv_sem=rs, device_id=to, device_id_type=MESH
        )

    def go(cp):
        cp.start()
        started.append(cp)

    def at_x(k):
        return FIRST[SHARED] + PER_X * lax.rem(x + NX + k, NX)

    def units(q):
        if q == SHARED:
            return pl.ds(at_x(0), PER_X)
        return pl.ds(FIRST[q], COUNT[q])

    main_rows = pl.ds(pl.multiple_of(z * MAIN, 16), MAIN)

    def z_copy(q, k):
        part = w.at[units(q), c, y, main_rows, :]
        return copy(part, part, z_s.at[q, k - 1], z_r.at[q, k - 1], z_peer(k))

    def t_copy(k):
        return copy(tail, tails.at[z], t_s.at[k - 1], t_r.at[k - 1], z_peer(k))

    def at_y(k):
        return lax.rem(y + NY + k, NY)

    def y_copy(q, i):
        part = w.at[units(q), c, y]
        if i == 2:
            part = w.at[units(q), c, at_y(-1), pl.ds(0, 80), :]
        if i == 3:
            part = w.at[units(q), c, at_y(1), pl.ds(80, 64), :]
        return copy(part, part, y_s.at[q, i], y_r.at[q, i], y_peer(1 if i % 2 == 0 else 3))

    def x_copy(i):
        if i < 2:
            part = w.at[units(SHARED), c]
        else:
            part = w.at[pl.ds(at_x(-1 if i == 2 else 1), PER_X), c, pl.ds(2 * (i - 2), 2)]
        return copy(part, part, x_s.at[i], x_r.at[i], x_peer(1 if i % 2 == 0 else 3))

    def c_copy(q, i):
        step = (0, -1, 1, 2)[i]
        part = w.at[pl.ds(at_x(step), PER_X), c] if q == SHARED else w.at[units(q), c, at_y(step)]
        return copy(part, part, c_s.at[q, i], c_r.at[q, i], core_peer)

    other = s + 1 - 2 * zl

    def gather_copy(buf, ss, rs, i):
        slot = s
        if i in (3, 4):
            slot = other
        if i == 5:
            slot = 2 * lax.rem(x + 3, NX) + zl
        if i == 6:
            slot = 2 * lax.rem(x + 1, NX) + 1 - zl
        rows = pl.ds(0, D)
        if i in (1, 2):
            rows = pl.ds(0, D // 2)
        if i in (7, 8):
            rows = pl.ds(D // 2, D // 2)
        to = pair if i == 0 else x_peer(1 if i % 2 == 1 else 3)
        part = buf.at[rows, lanes(slot)]
        return copy(part, part, ss.at[i], rs.at[i], to)

    def rows_copy(src, dst, ss, rs, k):
        to = lax.rem(s + k, NS)
        return copy(
            src.at[pl.ds(pl.multiple_of(to * 16, 16), 16), :],
            dst.at[pl.ds(pl.multiple_of(s * 16, 16), 16), :],
            ss.at[k - 1], rs.at[k - 1], s_peer(k),
        )

    def cols_copy(src, dst, n, ss, rs, k):
        to = lax.rem(s + k, NS)
        return copy(
            src.at[pl.ds(pl.multiple_of(to * n, 16), n), :], dst.at[:, lanes(s)],
            ss.at[k - 1], rs.at[k - 1], s_peer(k),
        )

    def sum_c(part, got, ss, rs):
        return copy(
            part.at[:, pl.ds(pl.multiple_of((1 - c) * 144, 16), 144), :], got, ss.at[0], rs.at[0], core_peer
        )

    def sum_y(half, got, ss, rs, k):
        return copy(half.at[lax.rem(y + k, NY)], got.at[k - 1], ss.at[k], rs.at[k], y_peer(k))

    def sum_z(slab, got, ss, rs, j):
        return copy(slab.at[j], got.at[z], ss.at[4 + j], rs.at[4 + z], (y * 8 + 4 * c + j, s))

    def add_c(part, got, half, ygot, ss, rs):
        sum_c(part, got, ss, rs).wait_recv()

        def body(b):
            own_half = part[b, pl.ds(pl.multiple_of(c * 144, 16), 144), :].astype(F32)
            half[b] = (own_half + got[b].astype(F32)).astype(BF)

        loop(NY, body)
        for k in range(1, NY):
            go(sum_y(half, ygot, ss, rs, k))

    def add_y(half, got, slab, zgot, ss, rs):
        for k in range(1, NY):
            sum_y(half, got, ss, rs, k).wait_recv()
        acc = half[y].astype(F32)
        for k in range(1, NY):
            acc += got[k - 1].astype(F32)
        for j in range(4):
            slab[j, 0:SHARD, :] = acc[SHARD * j : SHARD * j + SHARD].astype(BF)
            slab[j, SHARD:48, :] = jnp.zeros((48 - SHARD, acc.shape[1]), BF)
        for j in range(4):
            @pl.when(4 * c + j != u)
            def _():
                sum_z(slab, zgot, ss, rs, j).start()

            @pl.when(4 * c + j == u)
            def _():
                zgot[z] = slab[j]

    def add_z(slab, zgot, ss, rs, out):
        for zz in range(NZ):
            @pl.when((zz != z) | (u // 4 != c))
            def _():
                copy(slab.at[0], zgot.at[zz], ss.at[4], rs.at[4 + zz], core_peer).wait_recv()
        acc = zgot[0].astype(F32)
        for zz in range(1, NZ):
            acc += zgot[zz].astype(F32)
        out[...] = acc[0:SHARD]
        for j in range(4):
            @pl.when(4 * c + j != u)
            def _():
                sum_z(slab, zgot, ss, rs, j).wait_send()

    for cp in loads[:2]:
        cp.wait()
    pieces = []
    for ref in (wo, wi):
        rows = ref[MAIN:SHARD, :].astype(F32)
        pieces += [rows[:, j * TILE : j * TILE + TILE] for j in range(rows.shape[1] // TILE)]
    tail[...] = jnp.concatenate(pieces, axis=0).astype(BF)
    for n in range(9):
        w[n, c, y, main_rows, :] = wo[0:MAIN, n * TILE : n * TILE + TILE]
    for n in range(17, 36):
        w[n, c, y, main_rows, :] = wi[0:MAIN, (n - 9) * TILE : (n - 8) * TILE]
    for i in range(PER_X):
        w[at_x(0) + i, c, y, main_rows, :] = wi[0:MAIN, lanes(at_x(0) + i - 9)]
    tails[z] = tail[...]
    loads[2].wait()
    rows_to_t(qkv, spat, 3 * D, group=True)
    pl.semaphore_wait(barrier, len(peers))

    for k in range(1, NZ):
        go(t_copy(k))

    def z_start(q):
        for k in range(1, NZ):
            go(z_copy(q, k))

    z_start(SHARED)
    z_start(0)

    ki = lax.broadcasted_iota(jnp.int32, (T, T), 0)
    qi = lax.broadcasted_iota(jnp.int32, (T, T), 1)
    bias[...] = jnp.where((ki // 8) % 2 == (qi // 8) % 2, 0.0, -1e30).astype(F32)

    def half_attention(i):
        half = pl.ds(i * (D // 2), D // 2)
        attend(spat, bias, probs, ft, 8 * i, 8)
        mixed_all[half, lanes(s)] = ft[half, :].astype(BF)
        for j in (1, 2):
            go(gather_copy(mixed_all, mx_s, mx_r, j + 6 * i))

    half_attention(0)

    for k in range(1, NZ):
        t_copy(k).wait_recv()

    low = lax.broadcasted_iota(jnp.int32, (8, 128), 0) < 4

    def tail_tiles(m):
        full = [tails[zz, pl.ds(pl.multiple_of(m * 16, 16), 16), :].astype(F32) for zz in range(NZ)]
        tiles = []
        for half in range(2):
            a = [v[8 * half : 8 * half + 8] for v in full]
            r = [pltpu.roll(v, 4, 0) for v in a]
            even = [jnp.where(low, a[0], r[1]), jnp.where(low, a[2], r[3])]
            odd = [jnp.where(low, r[0], a[1]), jnp.where(low, r[2], a[3])]
            tiles += [jnp.concatenate(t, axis=0).astype(BF) for t in (even, odd)]
        return tiles

    for m in range(9):
        for i, tile in enumerate(tail_tiles(m)):
            n = 4 * m + i

            def put(n=n, tile=tile):
                w[n, c, y, pl.ds(NZ * MAIN, 16), :] = tile

            if FIRST[SHARED] <= n < FIRST[SHARED] + COUNT[SHARED]:
                pl.when(x == (n - FIRST[SHARED]) // PER_X)(put)
            else:
                put()

    def spread(q):
        for k in range(1, NZ):
            z_copy(q, k).wait_recv()
        go(y_copy(q, 0))
        go(y_copy(q, 1))
        if q != SHARED:
            go(c_copy(q, 0))

    def relay(q):
        for i in range(2):
            y_copy(q, i).wait_recv()
            go(y_copy(q, 2 + i))
            if q != SHARED:
                go(c_copy(q, 1 + i))

    def complete(q):
        for i in range(2):
            y_copy(q, 2 + i).wait_recv()
        if q == SHARED:
            go(x_copy(0))
            go(x_copy(1))
            go(c_copy(q, 0))
        else:
            go(c_copy(q, 3))

    def x_relay():
        for i in range(2):
            x_copy(i).wait_recv()
            go(x_copy(2 + i))
            go(c_copy(SHARED, 1 + i))

    def x_complete():
        for i in range(2):
            x_copy(2 + i).wait_recv()
        go(c_copy(SHARED, 3))

    def both_cores(q):
        for i in range(4):
            c_copy(q, i).wait_recv()

    def fan_own(buf, ss, rs):
        for i in (0, 1, 2, 7, 8):
            go(gather_copy(buf, ss, rs, i))

    def fan_other(buf, ss, rs):
        gather_copy(buf, ss, rs, 0).wait_recv()
        for i in (3, 4):
            go(gather_copy(buf, ss, rs, i))

    def pass_own(buf, ss, rs):
        for i in (1, 7):
            gather_copy(buf, ss, rs, i).wait_recv()
        go(gather_copy(buf, ss, rs, 5))

    def pass_other(buf, ss, rs):
        gather_copy(buf, ss, rs, 4).wait_recv()
        go(gather_copy(buf, ss, rs, 6))

    def fanned(buf, ss, rs):
        for i in (2, 8, 3, 5, 6):
            gather_copy(buf, ss, rs, i).wait_recv()

    def weight(n):
        return jnp.concatenate([w[n + i].reshape(D, TILE) for i in range(3)], axis=1)

    spread(SHARED)

    half_attention(1)
    z_start(1)
    z_start(2)
    go(gather_copy(mixed_all, mx_s, mx_r, 0))
    relay(SHARED)
    spread(0)
    permute(ft, fp)
    t_to_rows(fp, rows_b, D)
    loads[3].wait()
    loads[4].wait()
    complete(SHARED)
    bias[...] = jnp.where(ki % 8 == qi % 8, 0.0, -1e30).astype(F32)
    rows_to_t(gout, cot, D)
    pass_own(mixed_all, mx_s, mx_r)

    def swap_body(i):
        row = lax.broadcasted_iota(jnp.int32, (T, NS * T), 0) + i * T
        col = lax.broadcasted_iota(jnp.int32, (T, NS * T), 1)
        want = (((col >> 4) & 7) << 7) | ((col >> 7) << 4) | (col & 15)
        swap[rows8(i * T, T), :] = jnp.where(row == want, 1.0, 0.0).astype(BF)

    loop(NS, swap_body)
    relay(0)
    spread(1)
    x_relay()
    complete(0)
    both_cores(0)

    def hidden_body(n):
        tok = regroup(tokens[:, lanes(n, 384)].astype(F32))
        acc = contract(rows_b[...], weight(3 * n), 1, 0)
        hid[:, lanes(n, 384)] = (tok + acc).astype(BF)

    loop(3, hidden_body)
    own = pl.ds(pl.multiple_of(s * 16, 16), 16)
    hid_in[own, :] = hid[own, :]
    for k in range(1, NS):
        go(rows_copy(hid, hid_in, h_s, h_r, k))
    fan_other(mixed_all, mx_s, mx_r)
    spread(2)
    relay(1)
    x_complete()
    for k in range(1, NS):
        rows_copy(hid, hid_in, h_s, h_r, k).wait_recv()

    hf = hid_in[...].astype(F32)
    centred = hf - jnp.mean(hf, axis=-1, keepdims=True)
    inv = lax.rsqrt(jnp.mean(centred * centred, axis=-1, keepdims=True) + 1e-06)
    xh = centred * inv
    xhat[...] = xh
    rstd[...] = jnp.broadcast_to(inv, (T, 128))
    rows_t[...] = (xh * sc[...] + sh[...]).astype(BF).astype(F32)
    rows_to_t(rows_t, ft, D)
    mod_all[:, lanes(s)] = ft[...].astype(BF)
    fan_own(mod_all, md_s, md_r)
    permute(ft, fp)
    t_to_rows(fp, rows_b, D)

    def project(first, count):
        def body(i):
            acc = contract(rows_b[...], weight(first + 3 * i), 1, 0)
            packed[rows8((first - 9) * TILE + 3 * TILE * i, 3 * TILE), :] = acc.astype(BF).astype(F32).T

        loop(count, body)

    complete(1)
    relay(2)
    both_cores(SHARED)
    project(9, 2)
    both_cores(1)
    project(15, 4)
    fan_other(mod_all, md_s, md_r)
    attend(packed, bias, probs_t, None)
    complete(2)
    both_cores(2)
    project(27, 3)
    pass_own(mod_all, md_s, md_r)
    attend_back(packed, probs_t, cot, grad)
    grad_b[...] = grad[...].astype(BF)
    gt_all[:, lanes(s)] = grad_b[pl.ds(pl.multiple_of(s * 432, 16), 432), :]
    for k in range(1, NS):
        go(cols_copy(grad_b, gt_all, 432, gt_s, gt_r, k))
    pass_other(mod_all, md_s, md_r)

    def weight_t(n, b):
        return jnp.concatenate([w[n + i, b].reshape(576, TILE) for i in range(9)], axis=1)

    def back_body(b):
        acc = jnp.zeros((576, T), F32)
        for q in range(3):
            acc += contract(weight_t(9 + 9 * q, b), grad_b[pl.ds(q * D, D), :], 1, 0)
        fp[rows8(b * 576, 576), :] = acc

    loop(NC, back_body)
    unpermute(fp, ft)
    t_to_rows(ft, rows_t, D)
    dx = rows_t[...] * sc[...]
    xh = xhat[...]
    m1 = jnp.mean(dx, axis=-1, keepdims=True)
    m2 = jnp.mean(dx * xh, axis=-1, keepdims=True)
    g_out[...] = (rstd[:, 0:1] * (dx - m1 - xh * m2)).astype(BF)
    g_in[own, :] = g_out[own, :]
    for k in range(1, NS):
        go(rows_copy(g_out, g_in, g_s, g_r, k))
    pass_other(mixed_all, mx_s, mx_r)
    rows_to_t(g_out, gp_b, D)
    g_all[:, lanes(s)] = gp_b[pl.ds(pl.multiple_of(s * 144, 16), 144), :]
    for k in range(1, NS):
        go(cols_copy(gp_b, g_all, 144, gc_s, gc_r, k))

    fanned(mod_all, md_s, md_r)
    for k in range(1, NS):
        cols_copy(grad_b, gt_all, 432, gt_s, gt_r, k).wait_recv()

    def gwi_part(part, first, count):
        def body(b):
            part[b] = contract(mod_all[rows8(b * 288, 288), :], gt_all[pl.ds(first, count), :], 1, 1).astype(BF)

        loop(NY, body)

    gwi_part(gwa_p, 0, 256)
    go(sum_c(gwa_p, gwa_c, ra_s, ra_r))
    gwi_part(gwb_p, 256, 176)
    go(sum_c(gwb_p, gwb_c, rb_s, rb_r))

    for k in range(1, NS):
        rows_copy(g_out, g_in, g_s, g_r, k).wait_recv()
    rows_to_t(g_in, gt_b, D)

    def mixed_body(b):
        fp[rows8(b * 576, 576), :] = contract(weight_t(0, b), gt_b[...], 1, 0)

    loop(NC, mixed_body)
    unpermute(fp, ft)
    add_c(gwa_p, gwa_c, gwa_h, gwa_y, ra_s, ra_r)
    add_c(gwb_p, gwb_c, gwb_h, gwb_y, rb_s, rb_r)

    fanned(mixed_all, mx_s, mx_r)
    for k in range(1, NS):
        cols_copy(gp_b, g_all, 144, gc_s, gc_r, k).wait_recv()
    g_sorted = contract(g_all[...], swap[...], 1, 0).astype(BF)
    g_all[...] = g_sorted

    def gwo_body(b):
        gwo_p[b] = contract(mixed_all[rows8(b * 288, 288), :], g_all[...], 1, 1).astype(BF)

    loop(NY, gwo_body)
    go(sum_c(gwo_p, gwo_c, ro_s, ro_r))
    attend_back(spat, probs, ft, grad, 0, 8)
    add_c(gwo_p, gwo_c, gwo_h, gwo_y, ro_s, ro_r)
    add_y(gwa_h, gwa_y, gwa_t, gwa_z, ra_s, ra_r)
    attend_back(spat, probs, ft, grad, 8, 8)
    add_y(gwb_h, gwb_y, gwb_t, gwb_z, rb_s, rb_r)

    def qkv_body(j):
        out_qkv[:, lanes(j)] = ungroup(grad[rows8(j * 128, 128), :].T).astype(BF)

    loop(27, qkv_body)
    add_y(gwo_h, gwo_y, gwo_t, gwo_z, ro_s, ro_r)

    def out_body(j):
        out_tok[:, lanes(j)] = ungroup(g_in[:, lanes(j)].astype(F32)).astype(BF)

    loop(9, out_body)
    add_z(gwa_t, gwa_z, ra_s, ra_r, out_gwi.at[:, pl.ds(0, 256)])
    add_z(gwb_t, gwb_z, rb_s, rb_r, out_gwi.at[:, pl.ds(256, 176)])
    add_z(gwo_t, gwo_z, ro_s, ro_r, out_gwo)
    for cp in started:
        cp.wait_send()


def hand_over(*refs):
    for src, dst in zip(refs[:4], refs[4:]):
        dst[...] = src[...]


def time_modulation(timesteps):
    half = D // 2
    frequency = jnp.exp(-math.log(10000.0) * jnp.arange(half, dtype=F32) / half)
    angles = timesteps.astype(F32)[:, None] * frequency[None, :]
    cosine, sine = jnp.cos(angles), jnp.sin(angles)
    return (
        1.0 + 0.5 * jnp.concatenate([cosine, sine], axis=-1),
        0.5 * jnp.concatenate([sine, cosine], axis=-1),
    )


def shards(qkv_spatial, tokens, timesteps, w_out, w_in, grad_out):
    sc, sh = time_modulation(timesteps)
    dma = lambda *n: DMA(n)
    scratch = [
        VMEM((T, 3 * D), BF), VMEM((T, D), BF), VMEM((T, D), BF),
        VMEM((SHARD, D), BF), VMEM((SHARD, 3 * D), BF), VMEM((144, 128), BF),
        VMEM((36, NC, NY, BLOCK, TILE), BF),
        VMEM((NZ, 144, 128), BF),
        VMEM((3 * D, T), F32),
        VMEM((3 * D, T), F32),
        VMEM((HEADS, T, T), F32),
        VMEM((HEADS, T, T), F32),
        VMEM((T, T), F32),
        VMEM((3 * D, T), F32),
        VMEM((3 * D, T), BF),
        VMEM((D, T), F32),
        VMEM((D, T), F32),
        VMEM((T, D), BF),
        VMEM((T, D), F32),
        VMEM((T, D), BF),
        VMEM((T, D), BF),
        VMEM((T, D), BF),
        VMEM((T, D), F32),
        VMEM((T, 128), F32),
        VMEM((D, NS * T), BF),
        VMEM((D, NS * T), BF),
        VMEM((432, NS * T), BF),
        VMEM((144, NS * T), BF),
        VMEM((D, T), F32),
        VMEM((T, D), BF),
        VMEM((D, T), BF),
        VMEM((D, T), BF),
        VMEM((NS * T, NS * T), BF),
        *[VMEM(n + (m,), BF) for m in (256, 176, 144)
          for n in ((NY, 288), (NY, 144), (NY, 144), (3, 144), (4, 48), (4, 48))],
        dma(5), dma(4, 3), dma(4, 3), dma(3), dma(3), dma(4, 4), dma(4, 4), dma(4), dma(4), dma(4, 4), dma(4, 4),
        dma(9), dma(9), dma(9), dma(9),
        dma(7), dma(7), dma(7), dma(7), dma(7), dma(7), dma(7), dma(7),
        dma(8), dma(8), dma(8), dma(8), dma(8), dma(8),
    ]
    spec = pl.BlockSpec(memory_space=VMEM)
    results = pl.pallas_call(
        kernel,
        out_shape=(
            jax.ShapeDtypeStruct((T, 3 * D), BF),
            jax.ShapeDtypeStruct((T, D), BF),
            jax.ShapeDtypeStruct((SHARD, 144), F32),
            jax.ShapeDtypeStruct((SHARD, 432), F32),
        ),
        in_specs=[pl.BlockSpec(memory_space=pl.ANY)] * 5 + [spec] * 2,
        out_specs=(spec,) * 4,
        scratch_shapes=scratch,
        compiler_params=pltpu.CompilerParams(
            collective_id=0, has_side_effects=True, vmem_limit_bytes=60 * 1024 * 1024
        ),
    )(
        qkv_spatial.reshape(T, 3 * D), tokens.reshape(T, D), grad_out.reshape(T, D),
        w_out, w_in, sc, sh,
    )
    gq, gt, gwo, gwi = pl.pallas_call(
        hand_over,
        out_shape=tuple(jax.ShapeDtypeStruct(r.shape, r.dtype) for r in results),
        in_specs=[spec] * 4,
        out_specs=(spec,) * 4,
    )(*results)
    return gq.reshape(qkv_spatial.shape), gt.reshape(tokens.shape), gwo, gwi


def solution(mesh):
    placed = (
        P("dp", "seq", None, None),
        P("dp", "seq", None, None),
        P("dp"),
        P("dp", None),
        P("dp", None),
        P("dp", None, "seq", None),
    )
    return jax.shard_map(
        shards,
        mesh=mesh,
        in_specs=placed,
        out_specs=(
            P("dp", "seq", None, None),
            P("dp", "seq", None, None),
            P("dp", "seq"),
            P("dp", "seq"),
        ),
        check_vma=False,
    )
```
